32 devices in a mesh: src: 4 (over y, x), vox: 8 (over z, core).
Axes of the slice: x: 2, y: 2, z: 4, core: 2. Of those that a mesh axis runs over, the one named last changes fastest.
Arguments:
- kappa: float32 [64, 64, 256], P('vox'), may hold values from 0.3 to 3
- mua: float32 [64, 64, 256], P('vox'), may hold values from 0.1 to 2
- prior_forward_fields: float32 [8, 64, 64, 256], P('src', 'vox'), may hold values from -10 to 10
- prior_adjoint_fields: float32 [8, 64, 64, 256], P('src', 'vox'), may hold values from -10 to 10
- source_position: int32 [8], replicated, may hold values from 0 to 1048575
- detector_voxel: int32 [1024], P('vox'), may hold values from 0 to 1048575, as said below
- measured_source: int32 [32768], P(('src', 'vox')), may hold values from 0 to 7, as said below
- measured_detector: int32 [32768], P(('src', 'vox')), may hold values from 0 to 1023, as said below
- measured_data: float32 [32768], P(('src', 'vox')), may hold values from -6 to 6
- measured_weight: float32 [32768], P(('src', 'vox')), may hold values from 0.25 to 4
Outputs:
- grad_mua: float32 [64, 64, 256], P('vox', 'src')
- grad_kappa: float32 [64, 64, 256], P('vox', 'src')
The draws below stay inside these ranges and needn't reach their ends.
Inputs may be any that keep to these rules, and one draw needn't show every extreme that they name: `measured_source`: in each aligned block of 1024 rows (the rows of one device), at most 512 rows name a source of one group, a group being the 2 sources s with the same s // 2. `measured_detector`: row r names a detector of detector block (r // 1024) % 8, that is one from that block times 128 up to the next block's first. `detector_voxel`: detector d lies in the voxel planes x from (d // 128) * 8 to that plus 8 - 1.
All inputs are finite; a program needn't handle non-finite values.
Results may differ from the reference program's by a relative error of at most 0.0003.
Values sent between devices are 32-bit elements; how exact they have to be, the bound alone decides.
No kernel may reach another device: no remote copies, remote signals or barrier semaphores. Data moves between devices by JAX's collectives and lax.ppermute only.
A program may use at most 256 MiB of HBM per device.

```python
import math
import jax
import jax.numpy as jnp
from jax import lax

CX = 8
NY = 64
NZ = 256
SWEEPS = 6
SRC_DEV = 2
DET_DEV = 128
ROWS_DEV = 1024
NX = 64
NSRC = 8
DETECTOR_COUNT = 1024
MEASURE_ROWS = 32768


def draw_measured_source(key, part):
    block_count = MEASURE_ROWS // ROWS_DEV
    vox_count = DETECTOR_COUNT // DET_DEV
    group_count = NSRC // SRC_DEV
    slot_capacity = ROWS_DEV // 2
    key_busy, key_other, key_order, key_member = jax.random.split(key, 4)
    busiest = jax.random.randint(key_busy, (vox_count,), 0, group_count)
    column = jnp.arange(block_count) % vox_count
    block_busy = busiest[column]
    slots = jnp.arange(ROWS_DEV)
    others = jax.random.randint(key_other, (block_count, ROWS_DEV), 0, group_count - 1)
    others = others + (others >= block_busy[:, None]).astype(jnp.int32)
    chosen = jnp.where(slots[None, :] < slot_capacity, block_busy[:, None], others)
    scores = jax.random.randint(key_order, (block_count, ROWS_DEV), 0, 1 << 18) * ROWS_DEV + slots[None, :]
    order = jnp.argsort(scores, axis=1, stable=True)
    chosen = jnp.take_along_axis(chosen, order, axis=1)
    member = jax.random.randint(key_member, (block_count, ROWS_DEV), 0, SRC_DEV)
    return (chosen * SRC_DEV + member).reshape(-1).astype(jnp.int32)


def draw_measured_detector(key, part):
    vox_count = DETECTOR_COUNT // DET_DEV
    column = jnp.arange(MEASURE_ROWS) // ROWS_DEV % vox_count
    within = jax.random.randint(key, (MEASURE_ROWS,), 0, DET_DEV)
    return (column * DET_DEV + within).astype(jnp.int32)


def draw_detector_voxel(key, part):
    key_x, key_y, key_z = jax.random.split(key, 3)
    slab_position_index = jnp.arange(DETECTOR_COUNT) // DET_DEV
    plane_x = slab_position_index * CX + jax.random.randint(key_x, (DETECTOR_COUNT,), 0, CX)
    plane_y = jax.random.randint(key_y, (DETECTOR_COUNT,), 0, NY)
    plane_z = jax.random.randint(key_z, (DETECTOR_COUNT,), 0, NZ)
    return ((plane_x * NY + plane_y) * NZ + plane_z).astype(jnp.int32)


def set_ends(drawn, stream_key, low, top_value):
    longest = drawn.shape.index(max(drawn.shape))
    spots = []
    for shift in (0, 1):
        where = [jax.random.randint(jax.random.fold_in(stream_key, axis), (), 0, length) for axis, length in enumerate(drawn.shape)]
        where[longest] = (where[longest] + shift) % drawn.shape[longest]
        spots.append(tuple(where))
    return drawn.at[spots[0]].set(low).at[spots[1]].set(top_value)


def block_levels(key, extent, shards, low, high):
    factor_of, own = 1.0, jax.random.fold_in(key, 6)
    for position, parts in shards:
        steps = jnp.exp(jax.random.uniform(jax.random.fold_in(own, position), (parts,), jnp.float32, low / len(shards), high / len(shards)))
        factor_of = factor_of * jnp.repeat(steps, extent[position] // parts).reshape([-1 if axis == position else 1 for axis in range(len(extent))])
    return factor_of


def centred(rng, dims, width, limit, pieces=(), kind=jnp.bfloat16):
    result = width * jax.random.normal(rng, dims, jnp.float32)
    if pieces:
        result = result * block_levels(rng, dims, pieces, -0.22, 0.18)
    return jnp.clip(result, -limit, limit).astype(kind)


def setup_inputs(seed: int = 0) -> dict:
    keys = jax.random.split(jax.random.key(seed), 11)
    kappa = jnp.clip(jnp.exp(math.log(3.0) - 2.3025851 * jax.random.uniform(keys[0], (NX, NY, NZ), jnp.float32) ** block_levels(keys[0], (NX, NY, NZ), ((0, 8),), -0.2, 0.2)), 0.3, 3.0)
    mua = jnp.clip(jnp.exp(math.log(2.0) - 2.9957323 * jax.random.uniform(keys[1], (NX, NY, NZ), jnp.float32) ** block_levels(keys[1], (NX, NY, NZ), ((0, 8),), -0.2, 0.2)), 0.1, 2.0)
    prior_forward_fields = centred(keys[2], (NSRC, NX, NY, NZ), 2.0, 10.0, ((0, 4), (1, 8)), jnp.float32)
    prior_adjoint_fields = centred(keys[3], (NSRC, NX, NY, NZ), 2.0, 10.0, ((0, 4), (1, 8)), jnp.float32)
    source_position = set_ends(jax.random.randint(keys[4], (NSRC,), 0, NX * NY * NZ), jax.random.fold_in(keys[4], 1), 0, (NX * NY * NZ) - 1).astype(jnp.int32)
    detector_voxel = draw_detector_voxel(jax.random.fold_in(keys[10], 71), 0)
    measured_source = draw_measured_source(jax.random.fold_in(keys[10], 71), 0)
    measured_detector = draw_measured_detector(jax.random.fold_in(keys[10], 71), 0)
    measured_data = centred(keys[8], (MEASURE_ROWS,), 1.0, 6.0, ((0, 32),), jnp.float32)
    measured_weight = jnp.clip(jnp.exp(math.log(4.0) - 2.7725887 * jax.random.uniform(keys[9], (MEASURE_ROWS,), jnp.float32) ** block_levels(keys[9], (MEASURE_ROWS,), ((0, 32),), -0.2, 0.2)), 0.25, 4.0)
    return dict(kappa=kappa, mua=mua, prior_forward_fields=prior_forward_fields, prior_adjoint_fields=prior_adjoint_fields, source_position=source_position, detector_voxel=detector_voxel, measured_source=measured_source, measured_detector=measured_detector, measured_data=measured_data, measured_weight=measured_weight)


source_gain = 10.0


def conductances(kappa):
    padded = jnp.pad(kappa, 1)
    face_x = 0.5 * (padded[1:, 1:-1, 1:-1] + padded[:-1, 1:-1, 1:-1])
    face_y = 0.5 * (padded[1:-1, 1:, 1:-1] + padded[1:-1, :-1, 1:-1])
    face_z = 0.5 * (padded[1:-1, 1:-1, 1:] + padded[1:-1, 1:-1, :-1])
    return face_x, face_y, face_z


def jacobi_sweep(current, source, face_x, face_y, face_z, diagonal):
    padded = jnp.pad(current, 1)
    inflow = face_x[1:] * padded[2:, 1:-1, 1:-1] + face_x[:-1] * padded[:-2, 1:-1, 1:-1]
    inflow = inflow + face_y[:, 1:] * padded[1:-1, 2:, 1:-1] + face_y[:, :-1] * padded[1:-1, :-2, 1:-1]
    inflow = inflow + face_z[:, :, 1:] * padded[1:-1, 1:-1, 2:] + face_z[:, :, :-1] * padded[1:-1, 1:-1, :-2]
    return (source + inflow) / diagonal


def along(values, axis):
    upper = lax.slice_in_dim(values, 1, values.shape[axis], axis=axis)
    edge = jnp.zeros_like(lax.slice_in_dim(values, 0, 1, axis=axis))
    return jnp.concatenate([upper, edge], axis=axis) - values


def reference(kappa, mua, prior_forward_fields, prior_adjoint_fields, source_position, detector_voxel, measured_source, measured_detector, measured_data, measured_weight):
    face_x, face_y, face_z = conductances(kappa)
    diagonal = mua + face_x[1:] + face_x[:-1] + face_y[:, 1:] + face_y[:, :-1] + face_z[:, :, 1:] + face_z[:, :, :-1]
    cell_total = NX * NY * NZ

    def one_source(carry, inputs):
        grad_mua, grad_kappa = carry
        source_number, start_fwd, start_adj = inputs
        source = jnp.zeros((cell_total,), jnp.float32).at[source_position[source_number]].set(source_gain).reshape(NX, NY, NZ)
        forward = start_fwd
        for sweep in range(SWEEPS):
            forward = jacobi_sweep(forward, source, face_x, face_y, face_z, diagonal)
        predicted_value = forward.reshape(-1)[detector_voxel]
        residual_value = jnp.where(measured_source == source_number, measured_weight * (predicted_value[measured_detector] - measured_data), 0.0)
        detector_totals = jax.ops.segment_sum(residual_value, measured_detector, num_segments=DETECTOR_COUNT)
        back_source = jnp.zeros((cell_total,), jnp.float32).at[detector_voxel].add(detector_totals).reshape(NX, NY, NZ)
        adjoint = start_adj
        for sweep in range(SWEEPS):
            adjoint = jacobi_sweep(adjoint, back_source, face_x, face_y, face_z, diagonal)
        grad_mua = grad_mua - forward * adjoint
        product = along(forward, 0) * along(adjoint, 0) + along(forward, 1) * along(adjoint, 1) + along(forward, 2) * along(adjoint, 2)
        grad_kappa = grad_kappa - product
        return (grad_mua, grad_kappa), None

    zeros_grid = jnp.zeros((NX, NY, NZ), jnp.float32)
    source_ids = jnp.arange(NSRC, dtype=jnp.int32)
    (grad_mua, grad_kappa), unused = lax.scan(one_source, (zeros_grid, zeros_grid), (source_ids, prior_forward_fields, prior_adjoint_fields))
    return grad_mua, grad_kappa
```

```python
import functools

import jax
import jax.numpy as jnp
from jax import lax
from jax.experimental import pallas as pl
from jax.experimental.pallas import tpu as pltpu
from jax.sharding import PartitionSpec as P

SWEEPS = 6
HALO = SWEEPS + 1
LANES = 128
SUB = 8

source_gain = 10.0


def gather_planes(src, src_first, dst, dst_first, count):
    groups, chunks = src.shape[-2] // SUB, src.shape[-1] // LANES

    def step(i, carry):
        for y in range(0, groups * SUB, SUB):
            for j in range(chunks):
                part = src[src_first + i, pl.ds(y, SUB), pl.ds(LANES * j, LANES)]
                if groups == SUB:
                    dst[dst_first + i, j, pl.ds(y // SUB, SUB, stride=SUB), :] = part
                else:
                    for k in range(SUB):
                        row = (y + k) % groups * SUB + (y + k) // groups
                        dst[dst_first + i, j, pl.ds(row, 1), :] = part[k : k + 1]
        return carry

    lax.fori_loop(0, count, step, 0)


def lane_ids():
    return lax.broadcasted_iota(jnp.int32, (SUB, LANES), 1)


def sub_ids():
    return lax.broadcasted_iota(jnp.int32, (SUB, LANES), 0)


def next_z(chunks, lane):
    turned = [pltpu.roll(c, LANES - 1, 1) for c in chunks]
    return [jnp.where(lane == LANES - 1, turned[i + 1], turned[i]) if i + 1 < len(chunks) else turned[i] for i in range(len(chunks))]


def prev_z(chunks, lane):
    turned = [pltpu.roll(c, 1, 1) for c in chunks]
    return [jnp.where(lane == 0, turned[i - 1], turned[i]) if i > 0 else turned[i] for i in range(len(chunks))]


def load_rows(ref, lead, g, chunks):
    return [ref[(*lead, j, pl.ds(SUB * g, SUB), slice(None))] for j in range(chunks)]


def store_rows(ref, lead, g, values):
    for j, value in enumerate(values):
        ref[(*lead, j, pl.ds(SUB * g, SUB), slice(None))] = value


def coefficient_kernel(grid_planes, meta, kappa, mua, near, far, out, kap, mu):
    depth, width_y, width_z = kappa.shape
    groups, chunks = width_y // SUB, width_z // LANES
    lane, sub = lane_ids(), sub_ids()
    slab, parity = meta[0], meta[1]
    near_at = jnp.where(parity == 0, HALO + depth, 0)
    far_at = HALO + depth - near_at
    gather_planes(kappa, 0, kap, HALO, depth)
    gather_planes(near, 0, kap, near_at, HALO)
    gather_planes(far, 0, kap, far_at, HALO)
    mu_near = jnp.where(parity == 0, SWEEPS + depth, 0)
    mu_far = SWEEPS + depth - mu_near
    gather_planes(mua, 0, mu, SWEEPS, depth)
    gather_planes(near, HALO, mu, mu_near, SWEEPS)
    gather_planes(far, HALO, mu, mu_far, SWEEPS)

    def plane(i, carry):
        at = i + HALO - (SWEEPS - 1)
        place = slab * depth + i - (SWEEPS - 1)
        inside = jnp.logical_and(place >= 0, place < grid_planes)
        rows = [load_rows(kap, (at,), g, chunks) for g in range(groups)]
        for g in range(groups):
            mid = rows[g]
            low = load_rows(kap, (at - 1,), g, chunks)
            high = load_rows(kap, (at + 1,), g, chunks)
            if g > 0:
                before = rows[g - 1]
            else:
                before = [jnp.where(sub == 0, 0.0, pltpu.roll(c, 1, 0)) for c in rows[-1]]
            if g + 1 < groups:
                after = rows[g + 1]
            else:
                after = [jnp.where(sub == SUB - 1, 0.0, pltpu.roll(c, SUB - 1, 0)) for c in rows[0]]
            left = prev_z(mid, lane)
            left[0] = jnp.where(lane == 0, 0.0, left[0])
            right = next_z(mid, lane)
            right[-1] = jnp.where(lane == LANES - 1, 0.0, right[-1])
            absorb = load_rows(mu, (i + SWEEPS - (SWEEPS - 1),), g, chunks)
            for j in range(chunks):
                face = [0.5 * (mid[j] + other[j]) for other in (low, high, before, after, left, right)]
                diagonal = absorb[j] + face[0] + face[1] + face[2] + face[3] + face[4] + face[5]
                inverse = jnp.where(inside, 1.0 / diagonal, 0.0)
                if g == 0:
                    face[2] = jnp.where(sub == 0, 0.0, face[2])
                if g + 1 == groups:
                    face[3] = jnp.where(sub == SUB - 1, 0.0, face[3])
                if j == 0:
                    face[4] = jnp.where(lane == 0, 0.0, face[4])
                if j + 1 == chunks:
                    face[5] = jnp.where(lane == LANES - 1, 0.0, face[5])
                for k in range(6):
                    out[k, i, j, pl.ds(SUB * g, SUB), :] = face[k] * inverse
                out[6, i, j, pl.ds(SUB * g, SUB), :] = inverse
        return carry

    lax.fori_loop(0, depth + 2 * SWEEPS - 1, plane, 0)


def sweep_planes(coef, src, dst, first, last, bias):
    count, unused, chunks, width_y, lanes = src.shape
    groups = width_y // SUB
    lane = lane_ids()

    def plane(at, carry):
        c_at = at - (HALO - SWEEPS + 1)
        mids = [[load_rows(src, (s, at), g, chunks) for g in range(groups)] for s in range(count)]
        for g in range(groups):
            faces = [load_rows(coef, (k, c_at), g, chunks) for k in range(6)]
            for s in range(count):
                mid = mids[s][g]
                low = load_rows(src, (s, at - 1), g, chunks)
                high = load_rows(src, (s, at + 1), g, chunks)
                before = mids[s][g - 1] if g > 0 else [pltpu.roll(c, 1, 0) for c in mids[s][-1]]
                after = mids[s][g + 1] if g + 1 < groups else [pltpu.roll(c, SUB - 1, 0) for c in mids[s][0]]
                left, right = prev_z(mid, lane), next_z(mid, lane)
                result = []
                for j in range(chunks):
                    total = faces[0][j] * low[j] + faces[1][j] * high[j]
                    total = total + (faces[2][j] * before[j] + faces[3][j] * after[j])
                    total = total + (faces[4][j] * left[j] + faces[5][j] * right[j])
                    result.append(total)
                if bias is not None:
                    extra = load_rows(bias, (s, c_at), g, chunks)
                    result = [a + b for a, b in zip(result, extra)]
                store_rows(dst, (s, at), g, result)
        return carry

    lax.fori_loop(first + HALO, last + HALO + 1, plane, 0)


def detector_masks(cells, first, planes, width_y, width_z):
    groups = width_y // SUB
    y = cells // width_z % width_y
    row = (cells // (width_y * width_z) - first) * width_y + y % groups * SUB + y // groups
    row_at = lax.broadcasted_iota(jnp.int32, (planes * width_y, cells.shape[1]), 0)
    z_at = lax.broadcasted_iota(jnp.int32, (width_z, cells.shape[1]), 0)
    return row_at == row, z_at == cells % width_z


def split(values):
    high = values.astype(jnp.bfloat16)
    rest = values - high.astype(jnp.float32)
    middle = rest.astype(jnp.bfloat16)
    low = (rest - middle.astype(jnp.float32)).astype(jnp.bfloat16)
    return high, middle, low


def load_fields(meta, own, near, far, field):
    count, depth = own.shape[:2]
    near_at = jnp.where(meta[1] == 0, HALO + depth, 0)
    far_at = HALO + depth - near_at
    for s in range(count):
        gather_planes(own.at[s], 0, field.at[s], HALO, depth)
        gather_planes(near.at[s], 0, field.at[s], near_at, HALO)
        gather_planes(far.at[s], 0, field.at[s], far_at, HALO)


def forward_kernel(meta, coef, own, near, far, cells, totals, forward, adjoint_source, one, two):
    count, depth, width_y, width_z = own.shape
    groups = width_y // SUB
    slab = meta[0]
    load_fields(meta, own, near, far, one)
    src, dst = one, two
    for t in range(SWEEPS):
        reach = SWEEPS - 1 - t
        sweep_planes(coef, src, dst, -reach, depth + reach, None)
        for s in range(count):
            spot = meta[2 + s]
            p = spot // (width_y * width_z) - slab * depth
            y, z = spot // width_z % width_y, spot % width_z

            @pl.when(jnp.logical_and(p >= -reach, p <= depth + reach))
            def _():
                row = y % groups * SUB + y // groups
                tile = pl.multiple_of(row // SUB * SUB, SUB)
                at = (z // LANES, pl.ds(tile, SUB), slice(None))
                inverse = coef[(6, p + SWEEPS - 1, *at)]
                hit = jnp.logical_and(sub_ids() == row - tile, lane_ids() == z % LANES)
                old = dst[(s, p + HALO, *at)]
                dst[(s, p + HALO, *at)] = old + jnp.where(hit, source_gain * inverse, 0.0)

        src, dst = dst, src
    for s in range(count):
        forward[s] = src[s, pl.ds(HALO, depth + 1)]
    row_mask, z_mask = detector_masks(cells[...], 0, depth, width_y, width_z)
    z_hot = z_mask.astype(jnp.bfloat16)
    for s in range(count):
        sampled = 0.0
        for j in range(width_z // LANES):
            field = src[s, pl.ds(HALO, depth), j].reshape(depth * width_y, LANES)
            for part in split(field):
                sampled = sampled + jnp.dot(part, z_hot[LANES * j : LANES * (j + 1)], preferred_element_type=jnp.float32)
        predicted = jnp.sum(jnp.where(row_mask, sampled, 0.0), axis=0, keepdims=True)
        adjoint_source[pl.ds(s, 1), :] = predicted * totals[pl.ds(s, 1), :] - totals[pl.ds(count + s, 1), :]


def adjoint_kernel(
    meta, coef, own, near, far, forward, cells, source, near_cells, near_source, far_cells, far_source, grad_mua, grad_kappa, one, two, bias, plane_out
):
    count, depth, width_y, width_z = own.shape
    groups, chunks = width_y // SUB, width_z // LANES
    parity = meta[1]
    load_fields(meta, own, near, far, one)
    reach = SWEEPS - 1
    near_at = jnp.where(parity == 0, reach + depth, 0)
    far_at = jnp.where(parity == 0, 0, reach + depth)

    def add_sources(cell_ref, source_ref, at, planes, relative):
        row_mask, z_mask = detector_masks(cell_ref[...] + relative * (width_y * width_z), at, planes, width_y, width_z)
        z_hot = z_mask.astype(jnp.bfloat16)
        for s in range(count):
            spreads = [jnp.where(row_mask, part.astype(jnp.float32), 0.0).astype(jnp.bfloat16) for part in split(source_ref[pl.ds(s, 1), :])]
            for j in range(chunks):
                placed = 0.0
                for spread in spreads:
                    z_part = z_hot[LANES * j : LANES * (j + 1)]
                    placed = placed + lax.dot_general(spread, z_part, (((1,), (1,)), ((), ())), preferred_element_type=jnp.float32)
                placed = placed.reshape(planes, width_y, LANES)
                bias[s, pl.ds(at, planes), j] = placed * coef[6, pl.ds(at, planes), j]

    shift = jnp.where(parity == 0, depth, -depth)
    add_sources(near_cells, near_source, near_at, reach + 1, reach + shift)
    add_sources(far_cells, far_source, far_at, reach + 1, reach - shift)
    add_sources(cells, source, reach, depth, reach)
    src, dst = one, two
    for t in range(SWEEPS):
        reach = SWEEPS - 1 - t
        sweep_planes(coef, src, dst, -reach, depth + reach, bias)
        src, dst = dst, src
    lane, sub = lane_ids(), sub_ids()

    def steps(ref, s, at, mids, g):
        mid = mids[g]
        high = load_rows(ref, (s, at + 1), g, chunks)
        if g + 1 < groups:
            after = mids[g + 1]
        else:
            after = [jnp.where(sub == SUB - 1, 0.0, pltpu.roll(c, SUB - 1, 0)) for c in mids[0]]
        right = next_z(mid, lane)
        right[-1] = jnp.where(lane == LANES - 1, 0.0, right[-1])
        return [[other[j] - mid[j] for j in range(chunks)] for other in (high, after, right)]

    def plane(p, carry):
        mids_f = [[load_rows(forward, (s, p), g, chunks) for g in range(groups)] for s in range(count)]
        mids_a = [[load_rows(src, (s, p + HALO), g, chunks) for g in range(groups)] for s in range(count)]
        for g in range(groups):
            mua_sum, kappa_sum = [0.0] * chunks, [0.0] * chunks
            for s in range(count):
                d_f = steps(forward, s, p, mids_f[s], g)
                d_a = steps(src, s, p + HALO, mids_a[s], g)
                for j in range(chunks):
                    mua_sum[j] = mua_sum[j] - mids_f[s][g][j] * mids_a[s][g][j]
                    for a, b in zip(d_f, d_a):
                        kappa_sum[j] = kappa_sum[j] - a[j] * b[j]
            for j in range(chunks):
                plane_out[0, j, pl.ds(g, SUB, stride=groups), :] = mua_sum[j]
                plane_out[1, j, pl.ds(g, SUB, stride=groups), :] = kappa_sum[j]
        for j in range(chunks):
            grad_mua[p, :, pl.ds(LANES * j, LANES)] = plane_out[0, j]
            grad_kappa[p, :, pl.ds(LANES * j, LANES)] = plane_out[1, j]
        return carry

    lax.fori_loop(0, depth, plane, 0)


def measured_kernel(sources, detectors, data, weight, out):
    source_total = out.shape[0] // 2
    detector_count = out.shape[1]
    chunks, width = sources.shape
    total = jnp.zeros(out.shape, jnp.float32)
    detector_at = lax.broadcasted_iota(jnp.int32, (detector_count, width), 0)
    source_at = lax.broadcasted_iota(jnp.int32, (source_total, width), 0)
    for i in range(chunks):
        row = pl.ds(i, 1)
        hot = (detector_at == detectors[row, :]).astype(jnp.bfloat16)
        mine = source_at == sources[row, :]
        w = weight[row, :]
        left = jnp.concatenate([jnp.where(mine, w, 0.0), jnp.where(mine, w * data[row, :], 0.0)], axis=0)
        for part in split(left):
            total = total + lax.dot_general(part, hot, (((1,), (1,)), ((), ())), preferred_element_type=jnp.float32)
    out[...] = total


VMEM = pl.BlockSpec(memory_space=pltpu.VMEM)
SMEM = pl.BlockSpec(memory_space=pltpu.SMEM)


def call(kernel, outs, specs, scratch, *args):
    return pl.pallas_call(
        kernel,
        out_shape=outs,
        in_specs=specs,
        out_specs=jax.tree.map(lambda unused: VMEM, outs),
        scratch_shapes=scratch,
        compiler_params=pltpu.CompilerParams(vmem_limit_bytes=60 * 1024 * 1024),
    )(*args)


def near_swap(block, count):
    return lax.ppermute(block, "vox", [(i, i ^ 1) for i in range(count) if i ^ 1 < count])


def far_swap(block, count):
    pairs = [(i, i + 1) for i in range(1, count - 1, 2)]
    return lax.ppermute(block, "vox", pairs + [(b, a) for a, b in pairs])


def tile_sum(block, axis_name, order):
    count = lax.axis_size(axis_name)
    bits = count.bit_length() - 1
    me = lax.axis_index(axis_name)
    left = list(range(bits))
    for bit in order:
        dim = left.index(bit)
        shift = bits - 1 - bit
        mine = me >> shift & 1
        away = lax.dynamic_index_in_dim(block, 1 - mine, dim, False)
        kept = lax.dynamic_index_in_dim(block, mine, dim, False)
        block = kept + lax.ppermute(away, axis_name, [(i, i ^ (1 << shift)) for i in range(count)])
        left.remove(bit)
    return block


def body(
    kappa,
    mua,
    prior_forward_fields,
    prior_adjoint_fields,
    source_position,
    detector_voxel,
    measured_source,
    measured_detector,
    measured_data,
    measured_weight,
):
    count, depth, width_y, width_z = prior_forward_fields.shape
    plane_size = width_y * width_z
    slab, slabs = lax.axis_index("vox"), lax.axis_size("vox")
    group, groups = lax.axis_index("src"), lax.axis_size("src")
    parity = slab % 2
    detectors = detector_voxel.shape[0]
    f32 = jnp.float32

    def rims(block, dim, width, first):
        low = lax.slice_in_dim(block, 0, width, axis=dim)
        high = lax.slice_in_dim(block, block.shape[dim] - width, None, axis=dim)
        return jnp.where(parity == first, high, low)

    def coefficient_rims(first):
        return jnp.concatenate([rims(kappa, 0, HALO, first), rims(mua, 0, SWEEPS, first)], axis=0)

    coef_far = far_swap(coefficient_rims(1), slabs)
    coef_near = near_swap(coefficient_rims(0), slabs)
    fwd_far = far_swap(rims(prior_forward_fields, 1, HALO, 1), slabs)
    fwd_near = near_swap(rims(prior_forward_fields, 1, HALO, 0), slabs)
    adj_far = far_swap(rims(prior_adjoint_fields, 1, HALO, 1), slabs)
    adj_near = near_swap(rims(prior_adjoint_fields, 1, HALO, 0), slabs)

    cells = (detector_voxel - slab * depth * plane_size).reshape(1, detectors)
    cells_far = far_swap(cells, slabs)
    cells_near = near_swap(cells, slabs)

    rows = measured_source.shape[0]
    shaped = lambda a: a.reshape(rows // LANES, LANES)
    sums = call(
        measured_kernel,
        jax.ShapeDtypeStruct((2 * count * groups, detectors), f32),
        [VMEM] * 4,
        [],
        shaped(measured_source),
        shaped(measured_detector - slab * detectors),
        shaped(measured_data),
        shaped(measured_weight),
    )
    sums = sums.reshape(2, groups, count, detectors).transpose(1, 0, 2, 3).reshape(groups, 2 * count, detectors)
    totals = jnp.sum(lax.all_to_all(sums, "src", split_axis=0, concat_axis=0, tiled=True), axis=0)

    mine = lax.dynamic_slice_in_dim(source_position, group * count, count)
    meta = jnp.concatenate([jnp.stack([slab, parity]).astype(jnp.int32), mine])

    planes = depth + 2 * HALO
    plane = (width_z // LANES, width_y, LANES)
    coef = call(
        functools.partial(coefficient_kernel, depth * slabs),
        jax.ShapeDtypeStruct((7, depth + 2 * SWEEPS - 1, *plane), f32),
        [SMEM] + [VMEM] * 4,
        [pltpu.VMEM((planes, *plane), f32), pltpu.VMEM((planes - 2, *plane), f32)],
        meta,
        kappa,
        mua,
        coef_near,
        coef_far,
    )
    field = pltpu.VMEM((count, planes, *plane), f32)
    forward, source = call(
        forward_kernel,
        (
            jax.ShapeDtypeStruct((count, depth + 1, *plane), f32),
            jax.ShapeDtypeStruct((count, detectors), f32),
        ),
        [SMEM] + [VMEM] * 6,
        [field, field],
        meta,
        coef,
        prior_forward_fields,
        fwd_near,
        fwd_far,
        cells,
        totals,
    )
    source_far = far_swap(source, slabs)
    source_near = near_swap(source, slabs)
    grad_mua, grad_kappa = call(
        adjoint_kernel,
        (jax.ShapeDtypeStruct(kappa.shape, f32), jax.ShapeDtypeStruct(kappa.shape, f32)),
        [SMEM] + [VMEM] * 11,
        [field, field, pltpu.VMEM((count, depth + 2 * SWEEPS - 1, *plane), f32), pltpu.VMEM((2, *plane), f32)],
        meta,
        coef,
        prior_adjoint_fields,
        adj_near,
        adj_far,
        forward,
        cells,
        source,
        cells_near,
        source_near,
        cells_far,
        source_far,
    )
    bits = groups.bit_length() - 1

    def tiled(block):
        block = block.reshape(depth, groups, width_y // groups, width_z).transpose(1, 0, 2, 3)
        return block.reshape((2,) * bits + (depth, width_y // groups, width_z))

    return (
        tile_sum(tiled(grad_mua), "src", list(range(bits))),
        tile_sum(tiled(grad_kappa), "src", list(range(bits))[::-1]),
    )


def solution(mesh):
    in_specs = (
        P("vox", None, None),
        P("vox", None, None),
        P("src", "vox", None, None),
        P("src", "vox", None, None),
        P(),
        P("vox"),
        P(("src", "vox")),
        P(("src", "vox")),
        P(("src", "vox")),
        P(("src", "vox")),
    )
    out_specs = (P("vox", "src", None), P("vox", "src", None))
    return jax.shard_map(body, mesh=mesh, in_specs=in_specs, out_specs=out_specs, check_vma=False)
```

```python
import functools

import jax
import jax.numpy as jnp
from jax import lax
from jax.experimental import pallas as pl
from jax.experimental.pallas import tpu as pltpu
from jax.sharding import PartitionSpec as P

SWEEPS = 6
HALO = SWEEPS + 1
LANES = 128
SUB = 8

source_gain = 10.0


def lane_ids():
    return lax.broadcasted_iota(jnp.int32, (SUB, LANES), 1)


def sub_ids():
    return lax.broadcasted_iota(jnp.int32, (SUB, LANES), 0)


def next_z(chunks):
    return chunks[1:] + [pltpu.roll(chunks[0], LANES - 1, 1)]


def prev_z(chunks):
    return [pltpu.roll(chunks[-1], 1, 1)] + chunks[:-1]


def next_y(rows, g):
    return rows[g + 1] if g + 1 < len(rows) else [pltpu.roll(c, SUB - 1, 0) for c in rows[0]]


def prev_y(rows, g):
    return rows[g - 1] if g > 0 else [pltpu.roll(c, 1, 0) for c in rows[-1]]


def load_rows(ref, lead, g, chunks):
    return [ref[(*lead, j, pl.ds(SUB * g, SUB), slice(None))] for j in range(chunks)]


def load_plane(ref, lead, groups, chunks):
    return [load_rows(ref, lead, g, chunks) for g in range(groups)]


def store_rows(ref, lead, g, values):
    for j, value in enumerate(values):
        ref[(*lead, j, pl.ds(SUB * g, SUB), slice(None))] = value


def copy_planes(src, src_lead, src_first, dst, dst_lead, dst_first, count):
    for i in range(count):
        dst[(*dst_lead, dst_first + i)] = src[(*src_lead, src_first + i)]


def split(values):
    high = values.astype(jnp.bfloat16)
    rest = values - high.astype(jnp.float32)
    middle = rest.astype(jnp.bfloat16)
    low = (rest - middle.astype(jnp.float32)).astype(jnp.bfloat16)
    return high, middle, low


def z_order(width_z, natural_dim):
    chunks = width_z // LANES
    z = lax.broadcasted_iota(jnp.int32, (width_z, width_z), natural_dim)
    place = lax.broadcasted_iota(jnp.int32, (width_z, width_z), 1 - natural_dim)
    return (z == place % LANES * chunks + place // LANES).astype(jnp.bfloat16)


def pack_kernel(kinds, *refs):
    owns, (near, far) = refs[-2 - len(kinds) : -2], refs[-2:]
    blocks = []
    for ref in refs[: -2 - len(kinds)]:
        blocks += [ref] if ref.ndim == 3 else [ref.at[b] for b in range(ref.shape[0])]
    depth, width_y, width_z = blocks[0].shape
    chunks, groups = width_z // LANES, width_y // SUB
    parity = lax.axis_index("vox") % 2
    order = z_order(width_z, 0)
    together = 4
    at = 0
    for own, widths in zip(owns, kinds):
        for b, width in enumerate(widths):
            block = blocks.pop(0)
            for first in range(0, depth, together):
                values = block[pl.ds(first, together)].reshape(together * width_y, width_z)
                packed = sum(jnp.dot(part, order, preferred_element_type=jnp.float32) for part in split(values))
                for i in range(together):
                    for y in range(0, width_y, SUB):
                        for j in range(chunks):
                            part = packed[i * width_y + y : i * width_y + y + SUB, LANES * j : LANES * (j + 1)]
                            if groups == SUB:
                                own[b, first + i, j, pl.ds(y // SUB, SUB, stride=SUB), :] = part
                            else:
                                for k in range(SUB):
                                    row = (y + k) % groups * SUB + (y + k) // groups
                                    own[b, first + i, j, pl.ds(row, 1), :] = part[k : k + 1]
            low, high = 0, depth - width
            copy_planes(own, (b,), jnp.where(parity == 0, low, high), far, (), at, width)
            copy_planes(own, (b,), jnp.where(parity == 0, high, low), near, (), at, width)
            at += width


def early_part(t, depth, parity):
    return jnp.where(parity == 0, HALO + 1 + t, 1 + t), depth + HALO - 2 - 2 * t


def late_part(t, depth, parity):
    return jnp.where(parity == 0, 1 + t, depth + HALO - 1 - t), HALO


def halo_place(parity, near, depth, width):
    return jnp.where((parity == 0) == near, width + depth, 0)


def coefficient_planes(slab, kap, mu, out, first, count, depth):
    chunks, width_y = kap.shape[1:3]
    groups = width_y // SUB
    lane, sub = lane_ids(), sub_ids()
    grid_planes = lax.axis_size("vox") * depth

    def plane(n, carry):
        at = first + n
        i = at - (HALO - SWEEPS)
        place = slab * depth + i
        inside = jnp.logical_and(place >= SWEEPS, place < grid_planes + SWEEPS)
        rows = load_plane(kap, (at,), groups, chunks)
        for g in range(groups):
            mid = rows[g]
            low = load_rows(kap, (at - 1,), g, chunks)
            high = load_rows(kap, (at + 1,), g, chunks)
            before, after = prev_y(rows, g), next_y(rows, g)
            if g == 0:
                before = [jnp.where(sub == 0, 0.0, c) for c in before]
            if g + 1 == groups:
                after = [jnp.where(sub == SUB - 1, 0.0, c) for c in after]
            left, right = prev_z(mid), next_z(mid)
            left[0] = jnp.where(lane == 0, 0.0, left[0])
            right[-1] = jnp.where(lane == LANES - 1, 0.0, right[-1])
            absorb = load_rows(mu, (i,), g, chunks)
            for j in range(chunks):
                face = [0.5 * (mid[j] + other[j]) for other in (low, high, before, after, left, right)]
                diagonal = absorb[j] + face[0] + face[1] + face[2] + face[3] + face[4] + face[5]
                inverse = jnp.where(inside, 1.0 / diagonal, 0.0)
                if g == 0:
                    face[2] = jnp.where(sub == 0, 0.0, face[2])
                if g + 1 == groups:
                    face[3] = jnp.where(sub == SUB - 1, 0.0, face[3])
                if j == 0:
                    face[4] = jnp.where(lane == 0, 0.0, face[4])
                if j + 1 == chunks:
                    face[5] = jnp.where(lane == LANES - 1, 0.0, face[5])
                for k in range(6):
                    out[k, i, j, pl.ds(SUB * g, SUB), :] = face[k] * inverse
                out[6, i, j, pl.ds(SUB * g, SUB), :] = inverse
        return carry

    lax.fori_loop(0, count, plane, 0)


def sweep_planes(coef, src, dst, first, planes, bias):
    count, unused, chunks, width_y, lanes = src.shape
    groups = width_y // SUB

    def one(at):
        c_at = at - (HALO - SWEEPS)
        mids = [load_plane(src, (s, at), groups, chunks) for s in range(count)]
        for g in range(groups):
            faces = [load_rows(coef, (k, c_at), g, chunks) for k in range(6)]
            for s in range(count):
                mid = mids[s][g]
                low = load_rows(src, (s, at - 1), g, chunks)
                high = load_rows(src, (s, at + 1), g, chunks)
                before, after = prev_y(mids[s], g), next_y(mids[s], g)
                left, right = prev_z(mid), next_z(mid)
                result = []
                for j in range(chunks):
                    total = faces[0][j] * low[j] + faces[1][j] * high[j]
                    total = total + (faces[2][j] * before[j] + faces[3][j] * after[j])
                    total = total + (faces[4][j] * left[j] + faces[5][j] * right[j])
                    result.append(total)
                if bias is not None:
                    extra = load_rows(bias, (s, c_at), g, chunks)
                    result = [a + b for a, b in zip(result, extra)]
                store_rows(dst, (s, at), g, result)

    def pair(i, carry):
        one(first + 2 * i)
        one(first + 2 * i + 1)
        return carry

    lax.fori_loop(0, planes // 2, pair, 0)
    if planes % 2:
        one(first + planes - 1)


def detector_masks(cells, first, planes, width_y, width_z):
    groups, chunks = width_y // SUB, width_z // LANES
    y, z = cells // width_z % width_y, cells % width_z
    row = (cells // (width_y * width_z) - first) * width_y + y % groups * SUB + y // groups
    row_at = lax.broadcasted_iota(jnp.int32, (planes * width_y, cells.shape[1]), 0)
    lane_at = lax.broadcasted_iota(jnp.int32, (LANES, cells.shape[1]), 0)
    return row_at == row, [(lane_at * chunks + j == z).astype(jnp.bfloat16) for j in range(chunks)]


def forward_sweeps(part, positions, coef, one, two, depth):
    count, unused, chunks, width_y, lanes = one.shape
    width_z, groups = chunks * LANES, width_y // SUB
    slab, group = lax.axis_index("vox"), lax.axis_index("src")
    src, dst = one, two
    for t in range(SWEEPS):
        first, planes = part(t, depth, slab % 2)
        sweep_planes(coef, src, dst, first, planes, None)
        for s in range(count):
            spot = positions[group * count + s]
            at = spot // (width_y * width_z) + HALO - slab * depth
            y, z = spot // width_z % width_y, spot % width_z

            @pl.when(jnp.logical_and(at >= first, at < first + planes))
            def _():
                row = y % groups * SUB + y // groups
                tile = pl.multiple_of(row // SUB * SUB, SUB)
                where = (z % chunks, pl.ds(tile, SUB), slice(None))
                inverse = coef[(6, at - (HALO - SWEEPS), *where)]
                hit = jnp.logical_and(sub_ids() == row - tile, lane_ids() == z // chunks)
                old = dst[(s, at, *where)]
                dst[(s, at, *where)] = old + jnp.where(hit, source_gain * inverse, 0.0)

        src, dst = dst, src


def early_kernel(positions, coef_own, own, near, coef, one, two, kap, mu):
    count, depth = own.shape[:2]
    slab = lax.axis_index("vox")
    parity = slab % 2
    copy_planes(coef_own, (0,), 0, kap, (), HALO, depth)
    copy_planes(near, (), 0, kap, (), halo_place(parity, True, depth, HALO), HALO)
    copy_planes(coef_own, (1,), 0, mu, (), SWEEPS, depth)
    copy_planes(near, (), HALO, mu, (), halo_place(parity, True, depth, SWEEPS), SWEEPS)
    coefficient_planes(slab, kap, mu, coef, *early_part(0, depth, parity), depth)
    for s in range(count):
        copy_planes(own, (s,), 0, one, (s,), HALO, depth)
        copy_planes(near, (), HALO + SWEEPS + s * HALO, one, (s,), halo_place(parity, True, depth, HALO), HALO)
    forward_sweeps(early_part, positions, coef, one, two, depth)


def forward_kernel(positions, one_in, two_in, coef_in, coef_own, far, *rest):
    totals, (cells, one, two, coef, forward, adjoint_source, kap, mu) = rest[:-8], rest[-8:]
    count, planes, chunks, width_y = one.shape[:4]
    depth = planes - 2 * HALO
    width_z, groups = chunks * LANES, width_y // SUB
    slab = lax.axis_index("vox")
    parity = slab % 2
    copy_planes(coef_own, (0,), 0, kap, (), HALO, depth)
    copy_planes(far, (), 0, kap, (), halo_place(parity, False, depth, HALO), HALO)
    copy_planes(coef_own, (1,), 0, mu, (), SWEEPS, depth)
    copy_planes(far, (), HALO, mu, (), halo_place(parity, False, depth, SWEEPS), SWEEPS)
    coefficient_planes(slab, kap, mu, coef, *late_part(0, depth, parity), depth)
    for s in range(count):
        copy_planes(far, (), HALO + SWEEPS + s * HALO, one, (s,), halo_place(parity, False, depth, HALO), HALO)
    forward_sweeps(late_part, positions, coef, one, two, depth)
    for s in range(count):
        copy_planes(one, (s,), HALO, forward, (s,), 0, depth + 1)
    local_cells = cells[...] - slab * (depth * width_y * width_z)
    row_mask, z_hot = detector_masks(local_cells, 0, depth, width_y, width_z)
    total = sum(part[...] for part in totals)
    for s in range(count):
        sampled = 0.0
        for j in range(chunks):
            field = one[s, pl.ds(HALO, depth), j].reshape(depth * width_y, LANES)
            for part in split(field):
                sampled = sampled + jnp.dot(part, z_hot[j], preferred_element_type=jnp.float32)
        predicted = jnp.sum(jnp.where(row_mask, sampled, 0.0), axis=0, keepdims=True)
        adjoint_source[pl.ds(s, 1), :] = predicted * total[s : s + 1] - total[count + s : count + s + 1]
    adjoint_source[pl.ds(count, 1), :] = local_cells.astype(jnp.float32)


def adjoint_first_kernel(coef, own, near, one, two):
    count, depth = own.shape[:2]
    parity = lax.axis_index("vox") % 2
    for s in range(count):
        copy_planes(own, (s,), 0, one, (s,), HALO, depth)
        copy_planes(near, (), s * HALO, one, (s,), halo_place(parity, True, depth, HALO), HALO)
    sweep_planes(coef, one, two, *early_part(0, depth, parity), None)


def add_sources(coef, source, bias, at, planes, moved):
    count, unused, chunks, width_y, lanes = bias.shape
    width_z = chunks * LANES
    cells = source[pl.ds(count, 1), :].astype(jnp.int32) + moved * (width_y * width_z)
    row_mask, z_hot = detector_masks(cells, at, planes, width_y, width_z)
    for s in range(count):
        spreads = [jnp.where(row_mask, part.astype(jnp.float32), 0.0).astype(jnp.bfloat16) for part in split(source[pl.ds(s, 1), :])]
        for j in range(chunks):
            placed = 0.0
            for spread in spreads:
                placed = placed + lax.dot_general(spread, z_hot[j], (((1,), (1,)), ((), ())), preferred_element_type=jnp.float32)
            placed = placed.reshape(planes, width_y, LANES)
            bias[s, pl.ds(at, planes), j] = placed * coef[6, pl.ds(at, planes), j]


def adjoint_early_kernel(one_in, two_in, coef, source, near_source, one, two, bias):
    count, planes, chunks, width_y = one.shape[:4]
    depth = planes - 2 * HALO
    parity = lax.axis_index("vox") % 2
    moved = SWEEPS + jnp.where(parity == 0, depth, -depth)
    add_sources(coef, near_source, bias, halo_place(parity, True, depth, SWEEPS), SWEEPS, moved)
    add_sources(coef, source, bias, SWEEPS, depth, SWEEPS)
    first, count_first = early_part(0, depth, parity)

    def add(n, carry):
        at = first + n
        for s in range(count):
            two[s, at] = two[s, at] + bias[s, at - (HALO - SWEEPS)]
        return carry

    lax.fori_loop(0, count_first, add, 0)
    src, dst = two, one
    for t in range(1, SWEEPS):
        sweep_planes(coef, src, dst, *early_part(t, depth, parity), bias)
        src, dst = dst, src


def places(order):
    found = [0]
    for bit in reversed(order):
        found = found + [place | 1 << bit for place in found]
    return found


def adjoint_kernel(orders, one_in, two_in, bias_in, coef, far, forward, far_source, one, two, bias, *rest):
    outs, plane_out = rest[:-1], rest[-1]
    count, planes, chunks, width_y = one.shape[:4]
    depth = planes - 2 * HALO
    groups = width_y // SUB
    parity, group = lax.axis_index("vox") % 2, lax.axis_index("src")
    for s in range(count):
        copy_planes(far, (), s * HALO, one, (s,), halo_place(parity, False, depth, HALO), HALO)
    moved = SWEEPS - jnp.where(parity == 0, depth, -depth)
    add_sources(coef, far_source, bias, halo_place(parity, False, depth, SWEEPS), SWEEPS, moved)
    src, dst = one, two
    for t in range(SWEEPS):
        sweep_planes(coef, src, dst, *late_part(t, depth, parity), bias)
        src, dst = dst, src
    lane, sub = lane_ids(), sub_ids()

    def steps(ref, s, at, mids, g):
        mid = mids[g]
        high = load_rows(ref, (s, at + 1), g, chunks)
        after = next_y(mids, g)
        if g + 1 == groups:
            after = [jnp.where(sub == SUB - 1, 0.0, c) for c in after]
        right = next_z(mid)
        right[-1] = jnp.where(lane == LANES - 1, 0.0, right[-1])
        return [[other[j] - mid[j] for j in range(chunks)] for other in (high, after, right)]

    tiles = 1 << len(orders[0])
    tile_rows = width_y // tiles

    def plane(p, carry):
        mids_f = [load_plane(forward, (s, p), groups, chunks) for s in range(count)]
        mids_a = [load_plane(src, (s, p + HALO), groups, chunks) for s in range(count)]
        for g in range(groups):
            mua_sum, kappa_sum = [0.0] * chunks, [0.0] * chunks
            for s in range(count):
                d_f = steps(forward, s, p, mids_f[s], g)
                d_a = steps(src, s, p + HALO, mids_a[s], g)
                for j in range(chunks):
                    mua_sum[j] = mua_sum[j] - mids_f[s][g][j] * mids_a[s][g][j]
                    for a, b in zip(d_f, d_a):
                        kappa_sum[j] = kappa_sum[j] - a[j] * b[j]
            for j in range(chunks):
                plane_out[0, j, pl.ds(g, SUB, stride=groups), :] = mua_sum[j]
                plane_out[1, j, pl.ds(g, SUB, stride=groups), :] = kappa_sum[j]
        for k, order in enumerate(orders):
            for i, place in enumerate(places(order)):
                out = outs[2 * k + (0 if i < tiles // 2 else 1)]
                first = pl.multiple_of((group ^ place) * tile_rows, SUB)
                for j in range(chunks):
                    out[i % (tiles // 2), p, j] = plane_out[k, j, pl.ds(first, tile_rows), :]
        return carry

    lax.fori_loop(0, depth, plane, 0)


def unpack_kernel(*refs):
    pairs, outs = refs[: -len(refs) // 3], refs[-(len(refs) // 3) :]
    depth, chunks, rows, lanes = pairs[0].shape
    order = z_order(chunks * LANES, 1)
    for k, out in enumerate(outs):
        total = pairs[2 * k][...] + pairs[2 * k + 1][...]
        total = jnp.concatenate([total[:, j].reshape(depth * rows, LANES) for j in range(chunks)], axis=1)
        natural = sum(jnp.dot(part, order, preferred_element_type=jnp.float32) for part in split(total))
        out[...] = natural.reshape(out.shape)


def measured_kernel(count, sources, detectors, data, weight, *outs):
    kinds, detector_count = outs[0].shape
    chunks, width = sources.shape
    total = jnp.zeros((len(outs) * kinds, detector_count), jnp.float32)
    detector_at = lax.broadcasted_iota(jnp.int32, (detector_count, width), 0) + lax.axis_index("vox") * detector_count
    kind_at = lax.broadcasted_iota(jnp.int32, (len(outs) * kinds, width), 0)
    source_at = (kind_at // kinds ^ lax.axis_index("src")) * count + kind_at % count
    with_data = kind_at % kinds >= count
    for i in range(chunks):
        row = pl.ds(i, 1)
        hot = (detector_at == detectors[row, :]).astype(jnp.bfloat16)
        w = weight[row, :]
        left = jnp.where(source_at == sources[row, :], jnp.where(with_data, w * data[row, :], w), 0.0)
        for part in split(left):
            total = total + lax.dot_general(part, hot, (((1,), (1,)), ((), ())), preferred_element_type=jnp.float32)
    for d, out in enumerate(outs):
        out[...] = total[d * kinds : (d + 1) * kinds]


VMEM = pl.BlockSpec(memory_space=pltpu.VMEM)
SMEM = pl.BlockSpec(memory_space=pltpu.SMEM)


def held(*shape):
    return pltpu.VMEM(shape, jnp.float32)


def call(kernel, outs, scratch, limit, *args, raw=(), positions=None, kept=0, after=()):
    args = [pltpu.with_memory_space_constraint(a, pltpu.VMEM) for a in args]
    args += [pltpu.with_memory_space_constraint(a, pltpu.HBM) for a in raw]
    specs = [VMEM] * len(args)
    if after:
        inner, used = kernel, len(args) + (positions is not None)
        kernel = lambda *refs: inner(*refs[:used], *refs[used + len(after) :])
        args += [pltpu.with_memory_space_constraint(a, pltpu.VMEM) for a in after]
        specs += [VMEM] * len(after)
    shift = 0
    if positions is not None:
        args, specs = [positions, *args], [SMEM, *specs]
        shift = 1
    return pl.pallas_call(
        kernel,
        out_shape=outs,
        in_specs=specs,
        out_specs=[VMEM] * len(outs),
        scratch_shapes=scratch,
        input_output_aliases={k + shift: k for k in range(kept)},
        compiler_params=pltpu.CompilerParams(vmem_limit_bytes=limit * 1024 * 1024),
        cost_estimate=pl.CostEstimate(flops=1, bytes_accessed=1, transcendentals=0),
    )(*args)


def near_swap(block, count):
    return lax.ppermute(block, "vox", [(i, i ^ 1) for i in range(count) if i ^ 1 < count])


def far_swap(block, count):
    pairs = [(i, i + 1) for i in range(1, count - 1, 2)]
    return lax.ppermute(block, "vox", pairs + [(b, a) for a, b in pairs])


def body(
    kappa,
    mua,
    prior_forward_fields,
    prior_adjoint_fields,
    source_position,
    detector_voxel,
    measured_source,
    measured_detector,
    measured_data,
    measured_weight,
):
    count, depth, width_y, width_z = prior_forward_fields.shape
    slabs, groups = lax.axis_size("vox"), lax.axis_size("src")
    detectors = detector_voxel.shape[0]
    f32 = jnp.float32
    plane = (width_z // LANES, width_y, LANES)

    def pack(kinds, *blocks, after=()):
        rim = held(sum(sum(widths) for widths in kinds), *plane)
        outs = [held(len(widths), depth, *plane) for widths in kinds] + [rim, rim]
        return call(functools.partial(pack_kernel, kinds), outs, [], 6, raw=blocks, after=after)

    def sides(near, far):
        return near_swap(near, slabs), far_swap(far, slabs)

    planes = depth + 2 * HALO
    field = held(count, planes, *plane)
    coef_held = held(7, planes - 2, *plane)
    coef_work = [held(planes, *plane), held(planes - 2, *plane)]

    field_rims = (HALO,) * count
    coef_own, fwd_own, near, far = pack([(HALO, SWEEPS), field_rims], kappa, mua, prior_forward_fields)
    near, far = sides(near, far)
    adj_own, adj_near, adj_far = pack([field_rims], prior_adjoint_fields, after=[near])
    adj_near, adj_far = sides(adj_near, adj_far)
    coef, one, two = call(
        early_kernel,
        [coef_held, field, field],
        coef_work,
        6,
        coef_own,
        fwd_own,
        near,
        positions=source_position,
        after=[adj_near],
    )
    rows = measured_source.shape[0]
    sums = call(
        functools.partial(measured_kernel, count),
        [held(2 * count, detectors)] * groups,
        [],
        2,
        raw=[a.reshape(rows // LANES, LANES) for a in (measured_source, measured_detector, measured_data, measured_weight)],
        after=[adj_near],
    )
    totals = [sums[0]] + [lax.ppermute(sums[d], "src", [(i, i ^ d) for i in range(groups)]) for d in range(1, groups)]
    unused, unused, coef, forward, source = call(
        forward_kernel,
        [field, field, coef_held, held(count, depth + 1, *plane), held(count + 1, detectors)],
        coef_work,
        6,
        one,
        two,
        coef,
        coef_own,
        far,
        *totals,
        raw=[detector_voxel.reshape(1, detectors)],
        positions=source_position,
        kept=3,
    )
    source_near, source_far = sides(source, source)
    one, two = call(adjoint_first_kernel, [field, field], [], 3, coef, adj_own, adj_near, after=[source])
    one, two, bias = call(
        adjoint_early_kernel,
        [field, field, held(count, planes - 2, *plane)],
        [],
        6,
        one,
        two,
        coef,
        source,
        source_near,
        kept=2,
    )
    bits = list(range(groups.bit_length() - 1))
    orders = (bits, bits[::-1])
    half = held(groups // 2, depth, plane[0], width_y // groups, LANES)
    unused, unused, unused, *parts = call(
        functools.partial(adjoint_kernel, orders),
        [field, field, held(count, planes - 2, *plane)] + [half] * 4,
        [held(2, *plane)],
        6,
        one,
        two,
        bias,
        coef,
        adj_far,
        forward,
        source_far,
        kept=3,
    )

    def swap(block, bit):
        return lax.ppermute(block, "src", [(i, i ^ 1 << bit) for i in range(groups)])

    kept, sent = [parts[0], parts[2]], [parts[1], parts[3]]
    for step in range(len(bits)):
        got = [swap(sent[k], orders[k][step]) for k in range(2)]
        if step + 1 < len(bits):
            total = [kept[k] + got[k] for k in range(2)]
            middle = total[0].shape[0] // 2
            kept, sent = [t[:middle] for t in total], [t[middle:] for t in total]
    tile = jax.ShapeDtypeStruct((depth, width_y // groups, width_z), f32)
    return tuple(call(unpack_kernel, [tile, tile], [], 3, kept[0][0], got[0][0], kept[1][0], got[1][0]))


def solution(mesh):
    in_specs = (
        P("vox", None, None),
        P("vox", None, None),
        P("src", "vox", None, None),
        P("src", "vox", None, None),
        P(),
        P("vox"),
        P(("src", "vox")),
        P(("src", "vox")),
        P(("src", "vox")),
        P(("src", "vox")),
    )
    out_specs = (P("vox", "src", None), P("vox", "src", None))
    return jax.shard_map(body, mesh=mesh, in_specs=in_specs, out_specs=out_specs, check_vma=False)
```

```python
import functools

import jax
import jax.numpy as jnp
from jax import lax
from jax.experimental import pallas as pl
from jax.experimental.pallas import tpu as pltpu
from jax.sharding import PartitionSpec as P

SWEEPS = 6
HALO = SWEEPS + 1
LANES = 128
SUB = 8

source_gain = 10.0


def lane_ids():
    return lax.broadcasted_iota(jnp.int32, (SUB, LANES), 1)


def sub_ids():
    return lax.broadcasted_iota(jnp.int32, (SUB, LANES), 0)


def next_z(chunks):
    return chunks[1:] + [pltpu.roll(chunks[0], LANES - 1, 1)]


def prev_z(chunks):
    return [pltpu.roll(chunks[-1], 1, 1)] + chunks[:-1]


def next_y(rows, g):
    return rows[g + 1] if g + 1 < len(rows) else [pltpu.roll(c, SUB - 1, 0) for c in rows[0]]


def prev_y(rows, g):
    return rows[g - 1] if g > 0 else [pltpu.roll(c, 1, 0) for c in rows[-1]]


def load_rows(ref, lead, g, chunks):
    return [ref[(*lead, j, pl.ds(SUB * g, SUB), slice(None))] for j in range(chunks)]


def load_plane(ref, lead, groups, chunks):
    return [load_rows(ref, lead, g, chunks) for g in range(groups)]


def store_rows(ref, lead, g, values):
    for j, value in enumerate(values):
        ref[(*lead, j, pl.ds(SUB * g, SUB), slice(None))] = value


def copy_planes(src, src_lead, src_first, dst, dst_lead, dst_first, count):
    for i in range(count):
        dst[(*dst_lead, dst_first + i)] = src[(*src_lead, src_first + i)]


def split(values):
    high = values.astype(jnp.bfloat16)
    return high, (values - high.astype(jnp.float32)).astype(jnp.bfloat16)


def z_order(width_z, natural_dim):
    chunks = width_z // LANES
    z = lax.broadcasted_iota(jnp.int32, (width_z, width_z), natural_dim)
    place = lax.broadcasted_iota(jnp.int32, (width_z, width_z), 1 - natural_dim)
    return (z == place % LANES * chunks + place // LANES).astype(jnp.bfloat16)


def pack_kernel(kinds, *refs):
    (near, far, buffers, arrived), refs = refs[-4:], refs[:-4]
    owns, fetched = refs[-len(kinds) :], refs[: -len(kinds)]
    sources = []
    for ref in fetched:
        sources += [ref] if len(ref.shape) == 3 else [ref.at[b] for b in range(ref.shape[0])]
    copies = [pltpu.make_async_copy(ref, buffers.at[b], arrived.at[b]) for b, ref in enumerate(sources)]
    for copy in copies:
        copy.start()
    blocks = [buffers.at[b] for b in range(len(sources))]
    depth, width_y, width_z = buffers.shape[1:]
    chunks, groups = width_z // LANES, width_y // SUB
    parity = lax.axis_index("vox") % 2
    order = z_order(width_z, 0)
    together = 4
    at = 0
    for own, widths in zip(owns, kinds):
        for b, width in enumerate(widths):
            block = blocks.pop(0)
            copies.pop(0).wait()
            for first in range(0, depth, together):
                values = block[pl.ds(first, together)].reshape(together * width_y, width_z)
                packed = sum(jnp.dot(part, order, preferred_element_type=jnp.float32) for part in split(values))
                for i in range(together):
                    for y in range(0, width_y, SUB):
                        for j in range(chunks):
                            part = packed[i * width_y + y : i * width_y + y + SUB, LANES * j : LANES * (j + 1)]
                            if groups == SUB:
                                own[b, first + i, j, pl.ds(y // SUB, SUB, stride=SUB), :] = part
                            else:
                                for k in range(SUB):
                                    row = (y + k) % groups * SUB + (y + k) // groups
                                    own[b, first + i, j, pl.ds(row, 1), :] = part[k : k + 1]
            low, high = 0, depth - width
            copy_planes(own, (b,), jnp.where(parity == 0, low, high), far, (), at, width)
            copy_planes(own, (b,), jnp.where(parity == 0, high, low), near, (), at, width)
            at += width


def early_part(t, depth, parity):
    planes = depth + HALO - 2 - 2 * t
    more = 1 if t > 0 and planes % 4 == 3 else 0
    return jnp.where(parity == 0, HALO + 1 + t, 1 + t - more), planes + more


def late_part(t, depth, parity):
    return jnp.where(parity == 0, 1 + t, depth + HALO - 1 - t), HALO


def halo_place(parity, near, depth, width):
    return jnp.where((parity == 0) == near, width + depth, 0)


def coefficient_planes(slab, kap, mu, out, first, count, depth):
    chunks, width_y = kap.shape[1:3]
    groups = width_y // SUB
    lane, sub = lane_ids(), sub_ids()
    grid_planes = lax.axis_size("vox") * depth

    def plane(n, carry):
        at = first + n
        i = at - (HALO - SWEEPS)
        place = slab * depth + i
        inside = jnp.logical_and(place >= SWEEPS, place < grid_planes + SWEEPS)
        rows = load_plane(kap, (at,), groups, chunks)
        for g in range(groups):
            mid = rows[g]
            low = load_rows(kap, (at - 1,), g, chunks)
            high = load_rows(kap, (at + 1,), g, chunks)
            before, after = prev_y(rows, g), next_y(rows, g)
            if g == 0:
                before = [jnp.where(sub == 0, 0.0, c) for c in before]
            if g + 1 == groups:
                after = [jnp.where(sub == SUB - 1, 0.0, c) for c in after]
            left, right = prev_z(mid), next_z(mid)
            left[0] = jnp.where(lane == 0, 0.0, left[0])
            right[-1] = jnp.where(lane == LANES - 1, 0.0, right[-1])
            absorb = load_rows(mu, (i,), g, chunks)
            for j in range(chunks):
                face = [0.5 * (mid[j] + other[j]) for other in (low, high, before, after, left, right)]
                diagonal = absorb[j] + face[0] + face[1] + face[2] + face[3] + face[4] + face[5]
                inverse = jnp.where(inside, 1.0 / diagonal, 0.0)
                if g == 0:
                    face[2] = jnp.where(sub == 0, 0.0, face[2])
                if g + 1 == groups:
                    face[3] = jnp.where(sub == SUB - 1, 0.0, face[3])
                if j == 0:
                    face[4] = jnp.where(lane == 0, 0.0, face[4])
                if j + 1 == chunks:
                    face[5] = jnp.where(lane == LANES - 1, 0.0, face[5])
                for k in range(6):
                    out[k, i, j, pl.ds(SUB * g, SUB), :] = face[k] * inverse
                out[6, i, j, pl.ds(SUB * g, SUB), :] = inverse
        return carry

    lax.fori_loop(0, count, plane, 0)


def sweep_planes(coef, src, dst, first, planes, bias, together=4):
    count, unused, chunks, width_y, lanes = src.shape
    groups = width_y // SUB

    def one(at):
        c_at = at - (HALO - SWEEPS)
        for g in range(groups):
            faces = [load_rows(coef, (k, c_at), g, chunks) for k in range(6)]
            for s in range(count):
                rows = {h: load_rows(src, (s, at), h % groups, chunks) for h in (g - 1, g, g + 1)}
                mid = rows[g]
                low = load_rows(src, (s, at - 1), g, chunks)
                high = load_rows(src, (s, at + 1), g, chunks)
                before = rows[g - 1] if g > 0 else [pltpu.roll(c, 1, 0) for c in rows[g - 1]]
                after = rows[g + 1] if g + 1 < groups else [pltpu.roll(c, SUB - 1, 0) for c in rows[g + 1]]
                left, right = prev_z(mid), next_z(mid)
                result = []
                for j in range(chunks):
                    total = faces[0][j] * low[j] + faces[1][j] * high[j]
                    total = total + (faces[2][j] * before[j] + faces[3][j] * after[j])
                    total = total + (faces[4][j] * left[j] + faces[5][j] * right[j])
                    result.append(total)
                if bias is not None:
                    extra = load_rows(bias, (s, c_at), g, chunks)
                    result = [a + b for a, b in zip(result, extra)]
                store_rows(dst, (s, at), g, result)

    def several(i, carry):
        for k in range(together):
            one(first + together * i + k)
        return carry

    if planes >= together:
        lax.fori_loop(0, planes // together, several, 0)
    for k in range(planes // together * together, planes):
        one(first + k)


def detector_masks(cells, first, planes, width_y, width_z):
    groups, chunks = width_y // SUB, width_z // LANES
    y, z = cells // width_z % width_y, cells % width_z
    row = (cells // (width_y * width_z) - first) * width_y + y % groups * SUB + y // groups
    row_at = lax.broadcasted_iota(jnp.int32, (planes * width_y, cells.shape[1]), 0)
    lane_at = lax.broadcasted_iota(jnp.int32, (LANES, cells.shape[1]), 0)
    return row_at == row, [(lane_at * chunks + j == z).astype(jnp.bfloat16) for j in range(chunks)]


def find_sources(positions, spots, count, depth, chunks, width_y):
    width_z, groups = chunks * LANES, width_y // SUB
    slab, group = lax.axis_index("vox"), lax.axis_index("src")
    for s in range(count):
        spot = positions[group * count + s]
        y, z = spot // width_z % width_y, spot % width_z
        spots[s, 0] = spot // (width_y * width_z) + HALO - slab * depth
        spots[s, 1] = z % chunks
        spots[s, 2] = y % groups
        spots[s, 3] = y // groups
        spots[s, 4] = z // chunks


def forward_sweep(part, spots, coef, src, dst, t, depth, together):
    parity = lax.axis_index("vox") % 2
    first, planes = part(t, depth, parity)
    sweep_planes(coef, src, dst, first, planes, None, together)
    for s in range(src.shape[0]):
        at = spots[s, 0]

        @pl.when(jnp.logical_and(at >= first, at < first + planes))
        def _():
            where = (spots[s, 1], pl.ds(pl.multiple_of(spots[s, 2] * SUB, SUB), SUB), slice(None))
            inverse = coef[(6, at - (HALO - SWEEPS), *where)]
            hit = jnp.logical_and(sub_ids() == spots[s, 3], lane_ids() == spots[s, 4])
            dst[(s, at, *where)] = dst[(s, at, *where)] + jnp.where(hit, source_gain * inverse, 0.0)


def early_sweeps(sweep, one, two, begin):
    for t in range(begin, SWEEPS):
        src, dst = (one, two) if t % 2 == 0 else (two, one)
        sweep(early_part, src, dst, t, 4)


def late_sweeps(sweep, one, two):
    def step(i, carry):
        sweep(late_part, one, two, 2 * i, HALO)
        sweep(late_part, two, one, 2 * i + 1, HALO)
        return carry

    lax.fori_loop(0, SWEEPS // 2, step, 0)


def early_kernel(positions, coef_own, own, near, coef, one, two, kap, mu, spots):
    count, depth = own.shape[:2]
    slab = lax.axis_index("vox")
    parity = slab % 2
    copy_planes(coef_own, (0,), 0, kap, (), HALO, depth)
    copy_planes(near, (), 0, kap, (), halo_place(parity, True, depth, HALO), HALO)
    copy_planes(coef_own, (1,), 0, mu, (), SWEEPS, depth)
    copy_planes(near, (), HALO, mu, (), halo_place(parity, True, depth, SWEEPS), SWEEPS)
    coefficient_planes(slab, kap, mu, coef, *early_part(0, depth, parity), depth)
    for s in range(count):
        copy_planes(own, (s,), 0, one, (s,), HALO, depth)
        copy_planes(near, (), HALO + SWEEPS + s * HALO, one, (s,), halo_place(parity, True, depth, HALO), HALO)
    find_sources(positions, spots, count, depth, *own.shape[2:4])

    def sweep(part, src, dst, t, together):
        forward_sweep(part, spots, coef, src, dst, t, depth, together)

    early_sweeps(sweep, one, two, 0)


def forward_kernel(positions, one_in, two_in, coef_in, coef_own, far, *rest):
    totals, (cells, one, two, coef, forward, adjoint_source, kap, mu, spots) = rest[:-9], rest[-9:]
    count, planes, chunks, width_y = one.shape[:4]
    depth = planes - 2 * HALO
    width_z, groups = chunks * LANES, width_y // SUB
    slab = lax.axis_index("vox")
    parity = slab % 2
    copy_planes(coef_own, (0,), 0, kap, (), HALO, depth)
    copy_planes(far, (), 0, kap, (), halo_place(parity, False, depth, HALO), HALO)
    copy_planes(coef_own, (1,), 0, mu, (), SWEEPS, depth)
    copy_planes(far, (), HALO, mu, (), halo_place(parity, False, depth, SWEEPS), SWEEPS)
    coefficient_planes(slab, kap, mu, coef, *late_part(0, depth, parity), depth)
    for s in range(count):
        copy_planes(far, (), HALO + SWEEPS + s * HALO, one, (s,), halo_place(parity, False, depth, HALO), HALO)
    find_sources(positions, spots, count, depth, chunks, width_y)

    def sweep(part, src, dst, t, together):
        forward_sweep(part, spots, coef, src, dst, t, depth, together)

    late_sweeps(sweep, one, two)
    for s in range(count):
        copy_planes(one, (s,), HALO, forward, (s,), 0, depth + 1)
    local_cells = cells[...] - slab * (depth * width_y * width_z)
    row_mask, z_hot = detector_masks(local_cells, 0, depth, width_y, width_z)
    total = sum(part[...] for part in totals)
    for s in range(count):
        sampled = 0.0
        for j in range(chunks):
            field = one[s, pl.ds(HALO, depth), j].reshape(depth * width_y, LANES)
            for part in split(field):
                sampled = sampled + jnp.dot(part, z_hot[j], preferred_element_type=jnp.float32)
        predicted = jnp.sum(jnp.where(row_mask, sampled, 0.0), axis=0, keepdims=True)
        adjoint_source[pl.ds(s, 1), :] = predicted * total[s : s + 1] - total[count + s : count + s + 1]
    adjoint_source[pl.ds(count, 1), :] = local_cells.astype(jnp.float32)


def adjoint_first_kernel(coef, own, near, two, one):
    count, depth = own.shape[:2]
    parity = lax.axis_index("vox") % 2
    for s in range(count):
        copy_planes(own, (s,), 0, one, (s,), HALO, depth)
        copy_planes(near, (), s * HALO, one, (s,), halo_place(parity, True, depth, HALO), HALO)
    sweep_planes(coef, one, two, *early_part(0, depth, parity), None)


def add_sources(coef, source, bias, at, planes, moved):
    count, unused, chunks, width_y, lanes = bias.shape
    width_z = chunks * LANES
    cells = source[pl.ds(count, 1), :].astype(jnp.int32) + moved * (width_y * width_z)
    row_mask, z_hot = detector_masks(cells, at, planes, width_y, width_z)
    for s in range(count):
        spreads = [jnp.where(row_mask, part.astype(jnp.float32), 0.0).astype(jnp.bfloat16) for part in split(source[pl.ds(s, 1), :])]
        for j in range(chunks):
            placed = 0.0
            for spread in spreads:
                placed = placed + lax.dot_general(spread, z_hot[j], (((1,), (1,)), ((), ())), preferred_element_type=jnp.float32)
            placed = placed.reshape(planes, width_y, LANES)
            bias[s, pl.ds(at, planes), j] = placed * coef[6, pl.ds(at, planes), j]


def adjoint_early_kernel(two_in, coef, source, near_source, two, one, bias):
    count, planes, chunks, width_y = one.shape[:4]
    depth = planes - 2 * HALO
    parity = lax.axis_index("vox") % 2
    moved = SWEEPS + jnp.where(parity == 0, depth, -depth)
    add_sources(coef, near_source, bias, halo_place(parity, True, depth, SWEEPS), SWEEPS, moved)
    add_sources(coef, source, bias, SWEEPS, depth, SWEEPS)
    first, count_first = early_part(0, depth, parity)

    def add(n, carry):
        at = first + n
        for s in range(count):
            two[s, at] = two[s, at] + bias[s, at - (HALO - SWEEPS)]
        return carry

    lax.fori_loop(0, count_first, add, 0)

    def sweep(part, src, dst, t, together):
        sweep_planes(coef, src, dst, *part(t, depth, parity), bias, together)

    early_sweeps(sweep, one, two, 1)


def places(order):
    found = [0]
    for bit in reversed(order):
        found = found + [place | 1 << bit for place in found]
    return found


def adjoint_kernel(orders, one_in, two_in, bias_in, coef, own, far, forward, far_source, one, two, bias, *rest):
    outs, plane_out = rest[:-1], rest[-1]
    count, planes, chunks, width_y = one.shape[:4]
    depth = planes - 2 * HALO
    groups = width_y // SUB
    parity, group = lax.axis_index("vox") % 2, lax.axis_index("src")
    for s in range(count):
        copy_planes(far, (), s * HALO, one, (s,), halo_place(parity, False, depth, HALO), HALO)
        edge = jnp.where(parity == 0, 0, depth - 2)
        copy_planes(own, (s,), edge, one, (s,), edge + HALO, 2)
    moved = SWEEPS - jnp.where(parity == 0, depth, -depth)
    add_sources(coef, far_source, bias, halo_place(parity, False, depth, SWEEPS), SWEEPS, moved)

    def sweep(part, src, dst, t, together):
        sweep_planes(coef, src, dst, *part(t, depth, parity), bias, together)

    late_sweeps(sweep, one, two)
    src = one
    lane, sub = lane_ids(), sub_ids()

    def steps(ref, s, at, mids, g):
        mid = mids[g]
        high = load_rows(ref, (s, at + 1), g, chunks)
        after = next_y(mids, g)
        if g + 1 == groups:
            after = [jnp.where(sub == SUB - 1, 0.0, c) for c in after]
        right = next_z(mid)
        right[-1] = jnp.where(lane == LANES - 1, 0.0, right[-1])
        return [[other[j] - mid[j] for j in range(chunks)] for other in (high, after, right)]

    tiles = 1 << len(orders[0])
    tile_rows = width_y // tiles

    def plane(p, carry):
        mids_f = [load_plane(forward, (s, p), groups, chunks) for s in range(count)]
        mids_a = [load_plane(src, (s, p + HALO), groups, chunks) for s in range(count)]
        for g in range(groups):
            mua_sum, kappa_sum = [0.0] * chunks, [0.0] * chunks
            for s in range(count):
                d_f = steps(forward, s, p, mids_f[s], g)
                d_a = steps(src, s, p + HALO, mids_a[s], g)
                for j in range(chunks):
                    mua_sum[j] = mua_sum[j] - mids_f[s][g][j] * mids_a[s][g][j]
                    for a, b in zip(d_f, d_a):
                        kappa_sum[j] = kappa_sum[j] - a[j] * b[j]
            for j in range(chunks):
                plane_out[0, j, pl.ds(g, SUB, stride=groups), :] = mua_sum[j]
                plane_out[1, j, pl.ds(g, SUB, stride=groups), :] = kappa_sum[j]
        for k, order in enumerate(orders):
            for i, place in enumerate(places(order)):
                out = outs[2 * k + (0 if i < tiles // 2 else 1)]
                first = pl.multiple_of((group ^ place) * tile_rows, SUB)
                for j in range(chunks):
                    out[i % (tiles // 2), p, j] = plane_out[k, j, pl.ds(first, tile_rows), :]
        return carry

    lax.fori_loop(0, depth, plane, 0)


def unpack_kernel(*refs):
    pairs, outs = refs[: -len(refs) // 3], refs[-(len(refs) // 3) :]
    depth, chunks, rows, lanes = pairs[0].shape
    order = z_order(chunks * LANES, 1)
    for k, out in enumerate(outs):
        total = pairs[2 * k][...] + pairs[2 * k + 1][...]
        total = jnp.concatenate([total[:, j].reshape(depth * rows, LANES) for j in range(chunks)], axis=1)
        natural = sum(jnp.dot(part, order, preferred_element_type=jnp.float32) for part in split(total))
        out[...] = natural.reshape(out.shape)


def measured_kernel(count, sources, detectors, data, weight, *outs):
    kinds, detector_count = outs[0].shape
    chunks, width = sources.shape
    total = jnp.zeros((len(outs) * kinds, detector_count), jnp.float32)
    detector_at = lax.broadcasted_iota(jnp.int32, (detector_count, width), 0) + lax.axis_index("vox") * detector_count
    kind_at = lax.broadcasted_iota(jnp.int32, (len(outs) * kinds, width), 0)
    source_at = (kind_at // kinds ^ lax.axis_index("src")) * count + kind_at % count
    with_data = kind_at % kinds >= count
    for i in range(chunks):
        row = pl.ds(i, 1)
        hot = (detector_at == detectors[row, :]).astype(jnp.bfloat16)
        w = weight[row, :]
        left = jnp.where(source_at == sources[row, :], jnp.where(with_data, w * data[row, :], w), 0.0)
        for part in split(left):
            total = total + lax.dot_general(part, hot, (((1,), (1,)), ((), ())), preferred_element_type=jnp.float32)
    for d, out in enumerate(outs):
        out[...] = total[d * kinds : (d + 1) * kinds]


VMEM = pl.BlockSpec(memory_space=pltpu.VMEM)
SMEM = pl.BlockSpec(memory_space=pltpu.SMEM)


def held(*shape):
    return pltpu.VMEM(shape, jnp.float32)


def call(kernel, outs, scratch, limit, *args, raw=(), fetched=(), positions=None, kept=0, after=()):
    args = [pltpu.with_memory_space_constraint(a, pltpu.VMEM) for a in args]
    args += [pltpu.with_memory_space_constraint(a, pltpu.HBM) for a in raw]
    specs = [VMEM] * len(args)
    args += [pltpu.with_memory_space_constraint(a, pltpu.HBM) for a in fetched]
    specs += [pl.BlockSpec(memory_space=pltpu.HBM)] * len(fetched)
    if after:
        inner, used = kernel, len(args) + (positions is not None)
        kernel = lambda *refs: inner(*refs[:used], *refs[used + len(after) :])
        args += [pltpu.with_memory_space_constraint(a, pltpu.VMEM) for a in after]
        specs += [VMEM] * len(after)
    shift = 0
    if positions is not None:
        args, specs = [positions, *args], [SMEM, *specs]
        shift = 1
    return pl.pallas_call(
        kernel,
        out_shape=outs,
        in_specs=specs,
        out_specs=[VMEM] * len(outs),
        scratch_shapes=scratch,
        input_output_aliases={k + shift: k for k in range(kept)},
        compiler_params=pltpu.CompilerParams(vmem_limit_bytes=limit * 1024 * 1024),
        cost_estimate=pl.CostEstimate(flops=1, bytes_accessed=1, transcendentals=0),
    )(*args)


def near_swap(block, count):
    return lax.ppermute(block, "vox", [(i, i ^ 1) for i in range(count) if i ^ 1 < count])


def far_swap(block, count):
    pairs = [(i, i + 1) for i in range(1, count - 1, 2)]
    return lax.ppermute(block, "vox", pairs + [(b, a) for a, b in pairs])


def body(
    kappa,
    mua,
    prior_forward_fields,
    prior_adjoint_fields,
    source_position,
    detector_voxel,
    measured_source,
    measured_detector,
    measured_data,
    measured_weight,
):
    count, depth, width_y, width_z = prior_forward_fields.shape
    slabs, groups = lax.axis_size("vox"), lax.axis_size("src")
    detectors = detector_voxel.shape[0]
    f32 = jnp.float32
    plane = (width_z // LANES, width_y, LANES)

    def pack(kinds, *blocks, after=()):
        rim = held(sum(sum(widths) for widths in kinds), *plane)
        outs = [held(len(widths), depth, *plane) for widths in kinds] + [rim, rim]
        blocks_held = sum(len(widths) for widths in kinds)
        scratch = [held(blocks_held, depth, width_y, width_z), pltpu.SemaphoreType.DMA((blocks_held,))]
        return call(functools.partial(pack_kernel, kinds), outs, scratch, 6, fetched=blocks, after=after)

    def sides(near, far):
        return near_swap(near, slabs), far_swap(far, slabs)

    planes = depth + 2 * HALO
    field = held(count, planes, *plane)
    coef_held = held(7, planes - 2, *plane)
    coef_work = [held(planes, *plane), held(planes - 2, *plane)]

    field_rims = (HALO,) * count
    coef_own, fwd_own, near, far = pack([(HALO, SWEEPS), field_rims], kappa, mua, prior_forward_fields)
    near, far = sides(near, far)
    adj_own, adj_near, adj_far = pack([field_rims], prior_adjoint_fields, after=[near])
    adj_near, adj_far = sides(adj_near, adj_far)
    coef, one, two = call(
        early_kernel,
        [coef_held, field, field],
        [*coef_work, pltpu.SMEM((count, 5), jnp.int32)],
        6,
        coef_own,
        fwd_own,
        near,
        positions=source_position,
        after=[adj_near],
    )
    rows = measured_source.shape[0]
    sums = call(
        functools.partial(measured_kernel, count),
        [held(2 * count, detectors)] * groups,
        [],
        2,
        raw=[a.reshape(rows // LANES, LANES) for a in (measured_source, measured_detector, measured_data, measured_weight)],
        after=[adj_near],
    )
    totals = [sums[0]] + [lax.ppermute(sums[d], "src", [(i, i ^ d) for i in range(groups)]) for d in range(1, groups)]
    (adj_two,) = call(adjoint_first_kernel, [field], [field], 10, coef, adj_own, adj_near)
    unused, unused, coef, forward, source = call(
        forward_kernel,
        [field, field, coef_held, held(count, depth + 1, *plane), held(count + 1, detectors)],
        [*coef_work, pltpu.SMEM((count, 5), jnp.int32)],
        6,
        one,
        two,
        coef,
        coef_own,
        far,
        *totals,
        raw=[detector_voxel.reshape(1, detectors)],
        positions=source_position,
        kept=3,
        after=[adj_two],
    )
    source_near, source_far = sides(source, source)
    two, one, bias = call(
        adjoint_early_kernel,
        [field, field, held(count, planes - 2, *plane)],
        [],
        6,
        adj_two,
        coef,
        source,
        source_near,
        kept=1,
    )
    bits = list(range(groups.bit_length() - 1))
    orders = (bits, bits[::-1])
    half = held(groups // 2, depth, plane[0], width_y // groups, LANES)
    unused, unused, unused, *parts = call(
        functools.partial(adjoint_kernel, orders),
        [field, field, held(count, planes - 2, *plane)] + [half] * 4,
        [held(2, *plane)],
        6,
        one,
        two,
        bias,
        coef,
        adj_own,
        adj_far,
        forward,
        source_far,
        kept=3,
    )

    def swap(block, bit):
        return lax.ppermute(block, "src", [(i, i ^ 1 << bit) for i in range(groups)])

    kept, sent = [parts[0], parts[2]], [parts[1], parts[3]]
    for step in range(len(bits)):
        got = [swap(sent[k], orders[k][step]) for k in range(2)]
        if step + 1 < len(bits):
            total = [kept[k] + got[k] for k in range(2)]
            middle = total[0].shape[0] // 2
            kept, sent = [t[:middle] for t in total], [t[middle:] for t in total]
    tile = jax.ShapeDtypeStruct((depth, width_y // groups, width_z), f32)
    return tuple(call(unpack_kernel, [tile, tile], [], 3, kept[0][0], got[0][0], kept[1][0], got[1][0]))


def solution(mesh):
    in_specs = (
        P("vox", None, None),
        P("vox", None, None),
        P("src", "vox", None, None),
        P("src", "vox", None, None),
        P(),
        P("vox"),
        P(("src", "vox")),
        P(("src", "vox")),
        P(("src", "vox")),
        P(("src", "vox")),
    )
    out_specs = (P("vox", "src", None), P("vox", "src", None))
    return jax.shard_map(body, mesh=mesh, in_specs=in_specs, out_specs=out_specs, check_vma=False)
```

```python
import functools

import jax
import jax.numpy as jnp
from jax import lax
from jax.experimental import pallas as pl
from jax.experimental.pallas import tpu as pltpu
from jax.sharding import PartitionSpec as P

SWEEPS = 6
HALO = SWEEPS + 1
LANES = 128
SUB = 8

source_gain = 10.0


def lane_ids():
    return lax.broadcasted_iota(jnp.int32, (SUB, LANES), 1)


def sub_ids():
    return lax.broadcasted_iota(jnp.int32, (SUB, LANES), 0)


def next_z(chunks):
    return chunks[1:] + [pltpu.roll(chunks[0], LANES - 1, 1)]


def prev_z(chunks):
    return [pltpu.roll(chunks[-1], 1, 1)] + chunks[:-1]


def next_y(rows, g):
    return rows[g + 1] if g + 1 < len(rows) else [pltpu.roll(c, SUB - 1, 0) for c in rows[0]]


def prev_y(rows, g):
    return rows[g - 1] if g > 0 else [pltpu.roll(c, 1, 0) for c in rows[-1]]


def load_rows(ref, lead, g, chunks):
    return [ref[(*lead, j, pl.ds(SUB * g, SUB), slice(None))] for j in range(chunks)]


def load_plane(ref, lead, groups, chunks):
    return [load_rows(ref, lead, g, chunks) for g in range(groups)]


def store_rows(ref, lead, g, values):
    for j, value in enumerate(values):
        ref[(*lead, j, pl.ds(SUB * g, SUB), slice(None))] = value


def copy_planes(src, src_lead, src_first, dst, dst_lead, dst_first, count):
    for i in range(count):
        dst[(*dst_lead, dst_first + i)] = src[(*src_lead, src_first + i)]


def split(values):
    high = values.astype(jnp.bfloat16)
    return high, (values - high.astype(jnp.float32)).astype(jnp.bfloat16)


def exact_dot(values, hot, hot_dim):
    dims = (((1,), (hot_dim,)), ((), ()))
    return sum(lax.dot_general(part, hot, dims, preferred_element_type=jnp.float32) for part in split(values))


def z_order(width_z, natural_dim):
    chunks = width_z // LANES
    z = lax.broadcasted_iota(jnp.int32, (width_z, width_z), natural_dim)
    place = lax.broadcasted_iota(jnp.int32, (width_z, width_z), 1 - natural_dim)
    return (z == place % LANES * chunks + place // LANES).astype(jnp.bfloat16)


def pack_kernel(kinds, *refs):
    (near, far, buffers, arrived), refs = refs[-4:], refs[:-4]
    owns, fetched = refs[-len(kinds) :], refs[: -len(kinds)]
    sources = []
    for ref in fetched:
        sources += [ref] if len(ref.shape) == 3 else [ref.at[b] for b in range(ref.shape[0])]
    copies = [pltpu.make_async_copy(ref, buffers.at[b], arrived.at[b]) for b, ref in enumerate(sources)]
    for copy in copies:
        copy.start()
    blocks = [buffers.at[b] for b in range(len(sources))]
    depth, width_y, width_z = buffers.shape[1:]
    chunks, groups = width_z // LANES, width_y // SUB
    parity = lax.axis_index("vox") % 2
    order = z_order(width_z, 0)
    together = 4
    at = 0
    for own, widths in zip(owns, kinds):
        for b, width in enumerate(widths):
            block = blocks.pop(0)
            copies[0].wait()
            copies.pop(0)
            for first in range(0, depth, together):
                values = block[pl.ds(first, together)].reshape(together * width_y, width_z)
                packed = exact_dot(values, order, 0)
                for i in range(together):
                    for y in range(0, width_y, SUB):
                        for j in range(chunks):
                            part = packed[i * width_y + y : i * width_y + y + SUB, LANES * j : LANES * (j + 1)]
                            if groups == SUB:
                                own[b, first + i, j, pl.ds(y // SUB, SUB, stride=SUB), :] = part
                            else:
                                for k in range(SUB):
                                    row = (y + k) % groups * SUB + (y + k) // groups
                                    own[b, first + i, j, pl.ds(row, 1), :] = part[k : k + 1]
            low, high = 0, depth - width
            copy_planes(own, (b,), jnp.where(parity == 0, low, high), far, (), at, width)
            copy_planes(own, (b,), jnp.where(parity == 0, high, low), near, (), at, width)
            at += width


def early_part(t, depth, parity):
    planes = depth + HALO - 2 - 2 * t
    more = 1 if t > 0 and planes % 4 == 3 else 0
    return jnp.where(parity == 0, HALO + 1 + t, 1 + t - more), planes + more


def late_part(t, depth, parity):
    return jnp.where(parity == 0, 1 + t, depth + HALO - 1 - t), HALO


def halo_place(parity, near, depth, width):
    return jnp.where((parity == 0) == near, width + depth, 0)


def coefficient_planes(slab, kap, mu, out, first, count, depth):
    chunks, width_y = kap.shape[1:3]
    groups = width_y // SUB
    lane, sub = lane_ids(), sub_ids()
    grid_planes = lax.axis_size("vox") * depth

    def plane(n, carry):
        at = first + n
        i = at - (HALO - SWEEPS)
        place = slab * depth + i
        inside = jnp.logical_and(place >= SWEEPS, place < grid_planes + SWEEPS)
        rows = load_plane(kap, (at,), groups, chunks)
        for g in range(groups):
            mid = rows[g]
            low = load_rows(kap, (at - 1,), g, chunks)
            high = load_rows(kap, (at + 1,), g, chunks)
            before, after = prev_y(rows, g), next_y(rows, g)
            if g == 0:
                before = [jnp.where(sub == 0, 0.0, c) for c in before]
            if g + 1 == groups:
                after = [jnp.where(sub == SUB - 1, 0.0, c) for c in after]
            left, right = prev_z(mid), next_z(mid)
            left[0] = jnp.where(lane == 0, 0.0, left[0])
            right[-1] = jnp.where(lane == LANES - 1, 0.0, right[-1])
            absorb = load_rows(mu, (i,), g, chunks)
            for j in range(chunks):
                face = [0.5 * (mid[j] + other[j]) for other in (low, high, before, after, left, right)]
                diagonal = absorb[j] + face[0] + face[1] + face[2] + face[3] + face[4] + face[5]
                inverse = jnp.where(inside, 1.0 / diagonal, 0.0)
                if g == 0:
                    face[2] = jnp.where(sub == 0, 0.0, face[2])
                if g + 1 == groups:
                    face[3] = jnp.where(sub == SUB - 1, 0.0, face[3])
                if j == 0:
                    face[4] = jnp.where(lane == 0, 0.0, face[4])
                if j + 1 == chunks:
                    face[5] = jnp.where(lane == LANES - 1, 0.0, face[5])
                for k in range(6):
                    out[k, i, j, pl.ds(SUB * g, SUB), :] = face[k] * inverse
                out[6, i, j, pl.ds(SUB * g, SUB), :] = inverse
        return carry

    lax.fori_loop(0, count, plane, 0)


def sweep_planes(coef, src, dst, first, planes, bias, together=4):
    count, unused, chunks, width_y, lanes = src.shape
    groups = width_y // SUB

    def one(at):
        c_at = at - (HALO - SWEEPS)
        for g in range(groups):
            faces = [load_rows(coef, (k, c_at), g, chunks) for k in range(6)]
            for s in range(count):
                rows = {h: load_rows(src, (s, at), h % groups, chunks) for h in (g - 1, g, g + 1)}
                mid = rows[g]
                low = load_rows(src, (s, at - 1), g, chunks)
                high = load_rows(src, (s, at + 1), g, chunks)
                before = rows[g - 1] if g > 0 else [pltpu.roll(c, 1, 0) for c in rows[g - 1]]
                after = rows[g + 1] if g + 1 < groups else [pltpu.roll(c, SUB - 1, 0) for c in rows[g + 1]]
                left, right = prev_z(mid), next_z(mid)
                result = []
                for j in range(chunks):
                    total = faces[0][j] * low[j] + faces[1][j] * high[j]
                    total = total + (faces[2][j] * before[j] + faces[3][j] * after[j])
                    total = total + (faces[4][j] * left[j] + faces[5][j] * right[j])
                    result.append(total)
                if bias is not None:
                    extra = load_rows(bias, (s, c_at), g, chunks)
                    result = [a + b for a, b in zip(result, extra)]
                store_rows(dst, (s, at), g, result)

    def several(i, carry):
        for k in range(together):
            one(first + together * i + k)
        return carry

    if planes >= together:
        lax.fori_loop(0, planes // together, several, 0)
    for k in range(planes // together * together, planes):
        one(first + k)


def detector_masks(cells, first, planes, width_y, width_z):
    groups, chunks = width_y // SUB, width_z // LANES
    y, z = cells // width_z % width_y, cells % width_z
    row = (cells // (width_y * width_z) - first) * width_y + y % groups * SUB + y // groups
    row_at = lax.broadcasted_iota(jnp.int32, (planes * width_y, cells.shape[1]), 0)
    lane_at = lax.broadcasted_iota(jnp.int32, (LANES, cells.shape[1]), 0)
    return row_at == row, [(lane_at * chunks + j == z).astype(jnp.bfloat16) for j in range(chunks)]


def find_sources(positions, spots, count, depth, chunks, width_y):
    width_z, groups = chunks * LANES, width_y // SUB
    slab, group = lax.axis_index("vox"), lax.axis_index("src")
    for s in range(count):
        spot = positions[group * count + s]
        y, z = spot // width_z % width_y, spot % width_z
        spots[s, 0] = spot // (width_y * width_z) + HALO - slab * depth
        spots[s, 1] = z % chunks
        spots[s, 2] = y % groups
        spots[s, 3] = y // groups
        spots[s, 4] = z // chunks


def forward_sweep(part, spots, coef, src, dst, t, depth, together):
    parity = lax.axis_index("vox") % 2
    first, planes = part(t, depth, parity)
    sweep_planes(coef, src, dst, first, planes, None, together)
    for s in range(src.shape[0]):
        at = spots[s, 0]

        @pl.when(jnp.logical_and(at >= first, at < first + planes))
        def _():
            where = (spots[s, 1], pl.ds(pl.multiple_of(spots[s, 2] * SUB, SUB), SUB), slice(None))
            inverse = coef[(6, at - (HALO - SWEEPS), *where)]
            hit = jnp.logical_and(sub_ids() == spots[s, 3], lane_ids() == spots[s, 4])
            dst[(s, at, *where)] = dst[(s, at, *where)] + jnp.where(hit, source_gain * inverse, 0.0)


def early_sweeps(sweep, one, two, begin):
    for t in range(begin, SWEEPS):
        src, dst = (one, two) if t % 2 == 0 else (two, one)
        sweep(early_part, src, dst, t, 4)


def late_sweeps(sweep, one, two):
    def step(i, carry):
        sweep(late_part, one, two, 2 * i, HALO)
        sweep(late_part, two, one, 2 * i + 1, HALO)
        return carry

    lax.fori_loop(0, SWEEPS // 2, step, 0)


def early_kernel(positions, coef_own, own, near, coef, one, two, kap, mu, spots):
    count, depth = own.shape[:2]
    slab = lax.axis_index("vox")
    parity = slab % 2
    copy_planes(coef_own, (0,), 0, kap, (), HALO, depth)
    copy_planes(near, (), 0, kap, (), halo_place(parity, True, depth, HALO), HALO)
    copy_planes(coef_own, (1,), 0, mu, (), SWEEPS, depth)
    copy_planes(near, (), HALO, mu, (), halo_place(parity, True, depth, SWEEPS), SWEEPS)
    coefficient_planes(slab, kap, mu, coef, *early_part(0, depth, parity), depth)
    for s in range(count):
        copy_planes(own, (s,), 0, one, (s,), HALO, depth)
        copy_planes(near, (), HALO + SWEEPS + s * HALO, one, (s,), halo_place(parity, True, depth, HALO), HALO)
    find_sources(positions, spots, count, depth, *own.shape[2:4])

    def sweep(part, src, dst, t, together):
        forward_sweep(part, spots, coef, src, dst, t, depth, together)

    early_sweeps(sweep, one, two, 0)


def forward_kernel(positions, one_in, two_in, coef_in, coef_own, far, *rest):
    totals, (cells, one, two, coef, forward, adjoint_source, kap, mu, spots) = rest[:-9], rest[-9:]
    count, planes, chunks, width_y = one.shape[:4]
    depth = planes - 2 * HALO
    width_z, groups = chunks * LANES, width_y // SUB
    slab = lax.axis_index("vox")
    parity = slab % 2
    edge = jnp.where(parity == 0, 0, depth - 2)
    copy_planes(coef_own, (0,), edge, kap, (), edge + HALO, 2)
    copy_planes(far, (), 0, kap, (), halo_place(parity, False, depth, HALO), HALO)
    copy_planes(coef_own, (1,), edge, mu, (), edge + SWEEPS, 2)
    copy_planes(far, (), HALO, mu, (), halo_place(parity, False, depth, SWEEPS), SWEEPS)
    coefficient_planes(slab, kap, mu, coef, *late_part(0, depth, parity), depth)
    for s in range(count):
        copy_planes(far, (), HALO + SWEEPS + s * HALO, one, (s,), halo_place(parity, False, depth, HALO), HALO)
    find_sources(positions, spots, count, depth, chunks, width_y)

    def sweep(part, src, dst, t, together):
        forward_sweep(part, spots, coef, src, dst, t, depth, together)

    late_sweeps(sweep, one, two)
    for s in range(count):
        copy_planes(one, (s,), HALO, forward, (s,), 0, depth + 1)
    local_cells = cells[...] - slab * (depth * width_y * width_z)
    row_mask, z_hot = detector_masks(local_cells, 0, depth, width_y, width_z)
    total = sum(part[...] for part in totals)
    for s in range(count):
        field = [one[s, pl.ds(HALO, depth), j].reshape(depth * width_y, LANES) for j in range(chunks)]
        sampled = exact_dot(jnp.concatenate(field, axis=1), jnp.concatenate(z_hot, axis=0), 0)
        predicted = jnp.sum(jnp.where(row_mask, sampled, 0.0), axis=0, keepdims=True)
        adjoint_source[pl.ds(s, 1), :] = predicted * total[s : s + 1] - total[count + s : count + s + 1]
    adjoint_source[pl.ds(count, 1), :] = local_cells.astype(jnp.float32)


def adjoint_first_kernel(coef, own, near, two, one):
    count, depth = own.shape[:2]
    parity = lax.axis_index("vox") % 2
    for s in range(count):
        copy_planes(own, (s,), 0, one, (s,), HALO, depth)
        copy_planes(near, (), s * HALO, one, (s,), halo_place(parity, True, depth, HALO), HALO)
    sweep_planes(coef, one, two, *early_part(0, depth, parity), None)


def add_sources(coef, source, bias, at, planes, moved):
    count, unused, chunks, width_y, lanes = bias.shape
    width_z = chunks * LANES
    cells = source[pl.ds(count, 1), :].astype(jnp.int32) + moved * (width_y * width_z)
    row_mask, z_hot = detector_masks(cells, at, planes, width_y, width_z)
    for s in range(count):
        spreads = [jnp.where(row_mask, part.astype(jnp.float32), 0.0).astype(jnp.bfloat16) for part in split(source[pl.ds(s, 1), :])]
        for j in range(chunks):
            placed = 0.0
            for spread in spreads:
                placed = placed + lax.dot_general(spread, z_hot[j], (((1,), (1,)), ((), ())), preferred_element_type=jnp.float32)
            placed = placed.reshape(planes, width_y, LANES)
            bias[s, pl.ds(at, planes), j, pl.ds(0, width_y)] = placed * coef[6, pl.ds(at, planes), j, pl.ds(0, width_y)]


def adjoint_early_kernel(two_in, coef, source, near_source, two, one, bias):
    count, planes, chunks, width_y = one.shape[:4]
    depth = planes - 2 * HALO
    parity = lax.axis_index("vox") % 2
    moved = SWEEPS + jnp.where(parity == 0, depth, -depth)
    add_sources(coef, near_source, bias, halo_place(parity, True, depth, SWEEPS), SWEEPS, moved)
    add_sources(coef, source, bias, SWEEPS, depth, SWEEPS)
    first, count_first = early_part(0, depth, parity)

    def add(n, carry):
        at = first + n
        for s in range(count):
            two[s, at] = two[s, at] + bias[s, at - (HALO - SWEEPS)]
        return carry

    lax.fori_loop(0, count_first, add, 0)

    def sweep(part, src, dst, t, together):
        sweep_planes(coef, src, dst, *part(t, depth, parity), bias, together)

    early_sweeps(sweep, one, two, 1)


def places(order):
    found = [0]
    for bit in reversed(order):
        found = found + [place | 1 << bit for place in found]
    return found


def adjoint_kernel(orders, one_in, two_in, bias_in, coef, own, far, forward, far_source, one, two, bias, *rest):
    outs, plane_outs = rest[:-2], rest[-2:]
    count, planes, chunks, width_y = one.shape[:4]
    depth = planes - 2 * HALO
    groups = width_y // SUB
    parity, group = lax.axis_index("vox") % 2, lax.axis_index("src")
    for s in range(count):
        copy_planes(far, (), s * HALO, one, (s,), halo_place(parity, False, depth, HALO), HALO)
        edge = jnp.where(parity == 0, 0, depth - 2)
        copy_planes(own, (s,), edge, one, (s,), edge + HALO, 2)
    moved = SWEEPS - jnp.where(parity == 0, depth, -depth)
    add_sources(coef, far_source, bias, halo_place(parity, False, depth, SWEEPS), SWEEPS, moved)

    def sweep(part, src, dst, t, together):
        sweep_planes(coef, src, dst, *part(t, depth, parity), bias, together)

    late_sweeps(sweep, one, two)
    src = one
    lane, sub = lane_ids(), sub_ids()

    def steps(ref, s, at, mids, g):
        mid = mids[g]
        high = load_rows(ref, (s, at + 1), g, chunks)
        after = next_y(mids, g)
        if g + 1 == groups:
            after = [jnp.where(sub == SUB - 1, 0.0, c) for c in after]
        right = next_z(mid)
        right[-1] = jnp.where(lane == LANES - 1, 0.0, right[-1])
        return [[other[j] - mid[j] for j in range(chunks)] for other in (high, after, right)]

    tiles = 1 << len(orders[0])
    tile_rows = width_y // tiles

    def plane(p, plane_out):
        mids_f = [load_plane(forward, (s, p), groups, chunks) for s in range(count)]
        mids_a = [load_plane(src, (s, p + HALO), groups, chunks) for s in range(count)]
        for g in range(groups):
            mua_sum, kappa_sum = [0.0] * chunks, [0.0] * chunks
            for s in range(count):
                d_f = steps(forward, s, p, mids_f[s], g)
                d_a = steps(src, s, p + HALO, mids_a[s], g)
                for j in range(chunks):
                    mua_sum[j] = mua_sum[j] - mids_f[s][g][j] * mids_a[s][g][j]
                    for a, b in zip(d_f, d_a):
                        kappa_sum[j] = kappa_sum[j] - a[j] * b[j]
            for j in range(chunks):
                plane_out[0, j, pl.ds(g, SUB, stride=groups), :] = mua_sum[j]
                plane_out[1, j, pl.ds(g, SUB, stride=groups), :] = kappa_sum[j]
        for k, order in enumerate(orders):
            for i, place in enumerate(places(order)):
                out = outs[2 * k + (0 if i < tiles // 2 else 1)]
                first = pl.multiple_of((group ^ place) * tile_rows, SUB)
                for j in range(chunks):
                    out[i % (tiles // 2), p, j] = plane_out[k, j, pl.ds(first, tile_rows), :]

    def pair(i, carry):
        plane(2 * i, plane_outs[0])
        plane(2 * i + 1, plane_outs[1])
        return carry

    lax.fori_loop(0, depth // 2, pair, 0)


def unpack_kernel(*refs):
    pairs, outs = refs[: -len(refs) // 3], refs[-(len(refs) // 3) :]
    depth, chunks, rows, lanes = pairs[0].shape
    order = z_order(chunks * LANES, 1)
    for k, out in enumerate(outs):
        total = pairs[2 * k][...] + pairs[2 * k + 1][...]
        total = jnp.concatenate([total[:, j].reshape(depth * rows, LANES) for j in range(chunks)], axis=1)
        natural = exact_dot(total, order, 0)
        out[...] = natural.reshape(out.shape)


def measured_kernel(count, sources, detectors, data, weight, *outs):
    kinds, detector_count = outs[0].shape
    chunks, width = sources.shape
    total = jnp.zeros((len(outs) * kinds, detector_count), jnp.float32)
    detector_at = lax.broadcasted_iota(jnp.int32, (detector_count, width), 0) + lax.axis_index("vox") * detector_count
    kind_at = lax.broadcasted_iota(jnp.int32, (len(outs) * kinds, width), 0)
    source_at = (kind_at // kinds ^ lax.axis_index("src")) * count + kind_at % count
    with_data = kind_at % kinds >= count
    for i in range(chunks):
        row = pl.ds(i, 1)
        hot = (detector_at == detectors[row, :]).astype(jnp.bfloat16)
        w = weight[row, :]
        left = jnp.where(source_at == sources[row, :], jnp.where(with_data, w * data[row, :], w), 0.0)
        for part in split(left):
            total = total + lax.dot_general(part, hot, (((1,), (1,)), ((), ())), preferred_element_type=jnp.float32)
    for d, out in enumerate(outs):
        out[...] = total[d * kinds : (d + 1) * kinds]


VMEM = pl.BlockSpec(memory_space=pltpu.VMEM)
SMEM = pl.BlockSpec(memory_space=pltpu.SMEM)


def held(*shape):
    return pltpu.VMEM(shape, jnp.float32)


def call(kernel, outs, scratch, limit, *args, raw=(), fetched=(), positions=None, kept=0, after=()):
    args = [pltpu.with_memory_space_constraint(a, pltpu.VMEM) for a in args]
    args += [pltpu.with_memory_space_constraint(a, pltpu.HBM) for a in raw]
    specs = [VMEM] * len(args)
    args += [pltpu.with_memory_space_constraint(a, pltpu.HBM) for a in fetched]
    specs += [pl.BlockSpec(memory_space=pltpu.HBM)] * len(fetched)
    if after:
        inner, used = kernel, len(args) + (positions is not None)
        kernel = lambda *refs: inner(*refs[:used], *refs[used + len(after) :])
        args += [pltpu.with_memory_space_constraint(a, pltpu.VMEM) for a in after]
        specs += [VMEM] * len(after)
    shift = 0
    if positions is not None:
        args, specs = [positions, *args], [SMEM, *specs]
        shift = 1
    return pl.pallas_call(
        kernel,
        out_shape=outs,
        in_specs=specs,
        out_specs=[VMEM] * len(outs),
        scratch_shapes=scratch,
        input_output_aliases={k + shift: k for k in range(kept)},
        compiler_params=pltpu.CompilerParams(vmem_limit_bytes=limit * 1024 * 1024),
        cost_estimate=pl.CostEstimate(flops=1, bytes_accessed=1, transcendentals=0),
    )(*args)


def near_swap(block, count):
    return lax.ppermute(block, "vox", [(i, i ^ 1) for i in range(count) if i ^ 1 < count])


def far_swap(block, count):
    pairs = [(i, i + 1) for i in range(1, count - 1, 2)]
    return lax.ppermute(block, "vox", pairs + [(b, a) for a, b in pairs])


def body(
    kappa,
    mua,
    prior_forward_fields,
    prior_adjoint_fields,
    source_position,
    detector_voxel,
    measured_source,
    measured_detector,
    measured_data,
    measured_weight,
):
    count, depth, width_y, width_z = prior_forward_fields.shape
    slabs, groups = lax.axis_size("vox"), lax.axis_size("src")
    detectors = detector_voxel.shape[0]
    f32 = jnp.float32
    plane = (width_z // LANES, width_y, LANES)

    def pack(kinds, *blocks, after=()):
        rim = held(sum(sum(widths) for widths in kinds), *plane)
        outs = [held(len(widths), depth, *plane) for widths in kinds] + [rim, rim]
        blocks_held = sum(len(widths) for widths in kinds)
        scratch = [held(blocks_held, depth, width_y, width_z), pltpu.SemaphoreType.DMA((blocks_held,))]
        return call(functools.partial(pack_kernel, kinds), outs, scratch, 6, fetched=blocks, after=after)

    def sides(near, far):
        return near_swap(near, slabs), far_swap(far, slabs)

    planes = depth + 2 * HALO
    field = held(count, planes, *plane)
    padded = (plane[0], width_y + SUB, LANES)
    coef_held = held(7, planes - 2, *padded)
    coef_work = [held(planes, *plane), held(planes - 2, *plane)]

    field_rims = (HALO,) * count
    coef_own, fwd_own, near, far = pack([(HALO, SWEEPS), field_rims], kappa, mua, prior_forward_fields)
    near, far = sides(near, far)
    adj_own, adj_near, adj_far = pack([field_rims], prior_adjoint_fields, after=[near])
    adj_near, adj_far = sides(adj_near, adj_far)
    coef, one, two = call(
        early_kernel,
        [coef_held, field, field],
        [*coef_work, pltpu.SMEM((count, 5), jnp.int32)],
        6,
        coef_own,
        fwd_own,
        near,
        positions=source_position,
        after=[adj_near],
    )
    rows = measured_source.shape[0]
    sums = call(
        functools.partial(measured_kernel, count),
        [held(2 * count, detectors)] * groups,
        [],
        2,
        raw=[a.reshape(rows // LANES, LANES) for a in (measured_source, measured_detector, measured_data, measured_weight)],
        after=[adj_near],
    )
    totals = [sums[0]] + [lax.ppermute(sums[d], "src", [(i, i ^ d) for i in range(groups)]) for d in range(1, groups)]
    (adj_two,) = call(adjoint_first_kernel, [field], [field], 10, coef, adj_own, adj_near)
    unused, unused, coef, forward, source = call(
        forward_kernel,
        [field, field, coef_held, held(count, depth + 1, *plane), held(count + 1, detectors)],
        [*coef_work, pltpu.SMEM((count, 5), jnp.int32)],
        6,
        one,
        two,
        coef,
        coef_own,
        far,
        *totals,
        raw=[detector_voxel.reshape(1, detectors)],
        positions=source_position,
        kept=3,
        after=[adj_two],
    )
    source_near, source_far = sides(source, source)
    two, one, bias = call(
        adjoint_early_kernel,
        [field, field, held(count, planes - 2, *plane)],
        [],
        6,
        adj_two,
        coef,
        source,
        source_near,
        kept=1,
    )
    bits = list(range(groups.bit_length() - 1))
    orders = (bits, bits[::-1])
    half = held(groups // 2, depth, plane[0], width_y // groups, LANES)
    unused, unused, unused, *parts = call(
        functools.partial(adjoint_kernel, orders),
        [field, field, held(count, planes - 2, *plane)] + [half] * 4,
        [held(2, *plane)] * 2,
        6,
        one,
        two,
        bias,
        coef,
        adj_own,
        adj_far,
        forward,
        source_far,
        kept=3,
    )

    def swap(block, bit):
        return lax.ppermute(block, "src", [(i, i ^ 1 << bit) for i in range(groups)])

    kept, sent = [parts[0], parts[2]], [parts[1], parts[3]]
    for step in range(len(bits)):
        got = [swap(sent[k], orders[k][step]) for k in range(2)]
        if step + 1 < len(bits):
            total = [kept[k] + got[k] for k in range(2)]
            middle = total[0].shape[0] // 2
            kept, sent = [t[:middle] for t in total], [t[middle:] for t in total]
    tile = jax.ShapeDtypeStruct((depth, width_y // groups, width_z), f32)
    return tuple(call(unpack_kernel, [tile, tile], [], 3, kept[0][0], got[0][0], kept[1][0], got[1][0]))


def solution(mesh):
    in_specs = (
        P("vox", None, None),
        P("vox", None, None),
        P("src", "vox", None, None),
        P("src", "vox", None, None),
        P(),
        P("vox"),
        P(("src", "vox")),
        P(("src", "vox")),
        P(("src", "vox")),
        P(("src", "vox")),
    )
    out_specs = (P("vox", "src", None), P("vox", "src", None))
    return jax.shard_map(body, mesh=mesh, in_specs=in_specs, out_specs=out_specs, check_vma=False)
```

```python
import functools

import jax
import jax.numpy as jnp
from jax import lax
from jax.experimental import pallas as pl
from jax.experimental.pallas import tpu as pltpu
from jax.sharding import PartitionSpec as P

SWEEPS = 6
HALO = SWEEPS + 1
LANES = 128
SUB = 8

source_gain = 10.0


def lane_ids():
    return lax.broadcasted_iota(jnp.int32, (SUB, LANES), 1)


def sub_ids():
    return lax.broadcasted_iota(jnp.int32, (SUB, LANES), 0)


def next_z(chunks):
    return chunks[1:] + [pltpu.roll(chunks[0], LANES - 1, 1)]


def prev_z(chunks):
    return [pltpu.roll(chunks[-1], 1, 1)] + chunks[:-1]


def next_y(rows, g):
    return rows[g + 1] if g + 1 < len(rows) else [pltpu.roll(c, SUB - 1, 0) for c in rows[0]]


def prev_y(rows, g):
    return rows[g - 1] if g > 0 else [pltpu.roll(c, 1, 0) for c in rows[-1]]


def load_rows(ref, lead, g, chunks):
    return [ref[(*lead, j, pl.ds(SUB * g, SUB), slice(None))] for j in range(chunks)]


def load_plane(ref, lead, groups, chunks):
    return [load_rows(ref, lead, g, chunks) for g in range(groups)]


def store_rows(ref, lead, g, values):
    for j, value in enumerate(values):
        ref[(*lead, j, pl.ds(SUB * g, SUB), slice(None))] = value


def copy_planes(src, src_lead, src_first, dst, dst_lead, dst_first, count, scale=None):
    for i in range(count):
        plane = src[(*src_lead, src_first + i)]
        dst[(*dst_lead, dst_first + i)] = plane if scale is None else scale * plane


def split(values):
    high = values.astype(jnp.bfloat16)
    return high, (values - high.astype(jnp.float32)).astype(jnp.bfloat16)


def exact_dot(values, hot, hot_dim):
    dims = (((1,), (hot_dim,)), ((), ()))
    return sum(lax.dot_general(part, hot, dims, preferred_element_type=jnp.float32) for part in split(values))


def z_order(width_z, natural_dim):
    chunks = width_z // LANES
    z = lax.broadcasted_iota(jnp.int32, (width_z, width_z), natural_dim)
    place = lax.broadcasted_iota(jnp.int32, (width_z, width_z), 1 - natural_dim)
    return (z == place % LANES * chunks + place // LANES).astype(jnp.bfloat16)


def pack_kernel(kinds, *refs):
    (near, far, buffers, arrived), refs = refs[-4:], refs[:-4]
    owns, fetched = refs[-len(kinds) :], refs[: -len(kinds)]
    copies, first = [], 0
    for n, ref in enumerate(fetched):
        here = first if len(ref.shape) == 3 else pl.ds(first, ref.shape[0])
        copies.append((first, pltpu.make_async_copy(ref, buffers.at[here], arrived.at[n])))
        first += 1 if len(ref.shape) == 3 else ref.shape[0]
    for unused, copy in copies:
        copy.start()
    blocks = list(range(buffers.shape[0]))
    depth, width_y, width_z = buffers.shape[1:]
    chunks, groups = width_z // LANES, width_y // SUB
    parity = lax.axis_index("vox") % 2
    order = z_order(width_z, 0)
    together = 4
    at = 0
    for own, widths in zip(owns, kinds):
        for b, width in enumerate(widths):
            if copies and copies[0][0] == blocks[0]:
                copies.pop(0)[1].wait()
            block = buffers.at[blocks.pop(0)]
            for first in range(0, depth, together):
                values = block[pl.ds(first, together)].reshape(together * width_y, width_z)
                packed = exact_dot(values, order, 0)
                for i in range(together):
                    for y in range(0, width_y, SUB):
                        for j in range(chunks):
                            part = packed[i * width_y + y : i * width_y + y + SUB, LANES * j : LANES * (j + 1)]
                            if groups == SUB:
                                own[b, first + i, j, pl.ds(y // SUB, SUB, stride=SUB), :] = part
                            else:
                                for k in range(SUB):
                                    row = (y + k) % groups * SUB + (y + k) // groups
                                    own[b, first + i, j, pl.ds(row, 1), :] = part[k : k + 1]
            low, high = 0, depth - width
            copy_planes(own, (b,), jnp.where(parity == 0, low, high), far, (), at, width)
            copy_planes(own, (b,), jnp.where(parity == 0, high, low), near, (), at, width)
            at += width


def early_part(t, depth, parity):
    planes = depth + HALO - 2 - 2 * t
    more = 1 if t > 0 and planes % 4 == 3 else 0
    return jnp.where(parity == 0, HALO + 1 + t, 1 + t - more), planes + more


def late_part(t, depth, parity):
    return jnp.where(parity == 0, 1 + t, depth + HALO - 1 - t), HALO


def halo_place(parity, near, depth, width):
    return jnp.where((parity == 0) == near, width + depth, 0)


def coefficient_planes(slab, kap, mu, out, first, count, depth):
    chunks, width_y = kap.shape[1:3]
    groups = width_y // SUB
    lane, sub = lane_ids(), sub_ids()
    grid_planes = lax.axis_size("vox") * depth

    def plane(n, carry):
        at = first + n
        i = at - (HALO - SWEEPS)
        place = slab * depth + i
        inside = jnp.logical_and(place >= SWEEPS, place < grid_planes + SWEEPS)
        rows = load_plane(kap, (at,), groups, chunks)
        for g in range(groups):
            mid = rows[g]
            low = load_rows(kap, (at - 1,), g, chunks)
            high = load_rows(kap, (at + 1,), g, chunks)
            before, after = prev_y(rows, g), next_y(rows, g)
            if g == 0:
                before = [jnp.where(sub == 0, 0.0, c) for c in before]
            if g + 1 == groups:
                after = [jnp.where(sub == SUB - 1, 0.0, c) for c in after]
            left, right = prev_z(mid), next_z(mid)
            left[0] = jnp.where(lane == 0, 0.0, left[0])
            right[-1] = jnp.where(lane == LANES - 1, 0.0, right[-1])
            absorb = load_rows(mu, (i,), g, chunks)
            for j in range(chunks):
                face = [mid[j] + other[j] for other in (low, high, before, after, left, right)]
                diagonal = absorb[j] + face[0] + face[1] + face[2] + face[3] + face[4] + face[5]
                inverse = jnp.where(inside, 1.0 / diagonal, 0.0)
                if g == 0:
                    face[2] = jnp.where(sub == 0, 0.0, face[2])
                if g + 1 == groups:
                    face[3] = jnp.where(sub == SUB - 1, 0.0, face[3])
                if j == 0:
                    face[4] = jnp.where(lane == 0, 0.0, face[4])
                if j + 1 == chunks:
                    face[5] = jnp.where(lane == LANES - 1, 0.0, face[5])
                for k in range(6):
                    out[k, i, j, pl.ds(SUB * g, SUB), :] = face[k] * inverse
                out[6, i, j, pl.ds(SUB * g, SUB), :] = inverse
        return carry

    lax.fori_loop(0, count, plane, 0)


def sweep_planes(coef, src, dst, first, planes, bias, together=4):
    count, unused, chunks, width_y, lanes = src.shape
    groups = width_y // SUB

    def one(at):
        c_at = at - (HALO - SWEEPS)
        for g in range(groups):
            faces = [load_rows(coef, (k, c_at), g, chunks) for k in range(6)]
            for s in range(count):
                rows = {h: load_rows(src, (s, at), h % groups, chunks) for h in (g - 1, g, g + 1)}
                mid = rows[g]
                low = load_rows(src, (s, at - 1), g, chunks)
                high = load_rows(src, (s, at + 1), g, chunks)
                before = rows[g - 1] if g > 0 else [pltpu.roll(c, 1, 0) for c in rows[g - 1]]
                after = rows[g + 1] if g + 1 < groups else [pltpu.roll(c, SUB - 1, 0) for c in rows[g + 1]]
                left, right = prev_z(mid), next_z(mid)
                result = []
                for j in range(chunks):
                    total = faces[0][j] * low[j] + faces[1][j] * high[j]
                    total = total + (faces[2][j] * before[j] + faces[3][j] * after[j])
                    total = total + (faces[4][j] * left[j] + faces[5][j] * right[j])
                    result.append(total)
                if bias is not None:
                    extra = load_rows(bias, (s, c_at), g, chunks)
                    result = [a + b for a, b in zip(result, extra)]
                store_rows(dst, (s, at), g, result)

    def several(i, carry):
        for k in range(together):
            one(first + together * i + k)
        return carry

    if planes >= together:
        lax.fori_loop(0, planes // together, several, 0)
    for k in range(planes // together * together, planes):
        one(first + k)


def detector_masks(cells, first, planes, width_y, width_z):
    groups, chunks = width_y // SUB, width_z // LANES
    y, z = cells // width_z % width_y, cells % width_z
    row = (cells // (width_y * width_z) - first) * width_y + y % groups * SUB + y // groups
    row_at = lax.broadcasted_iota(jnp.int32, (planes * width_y, cells.shape[1]), 0)
    lane_at = lax.broadcasted_iota(jnp.int32, (LANES, cells.shape[1]), 0)
    return row_at == row, [(lane_at * chunks + j == z).astype(jnp.bfloat16) for j in range(chunks)]


def find_sources(positions, spots, count, depth, chunks, width_y):
    width_z, groups = chunks * LANES, width_y // SUB
    slab, group = lax.axis_index("vox"), lax.axis_index("src")
    for s in range(count):
        spot = positions[group * count + s]
        y, z = spot // width_z % width_y, spot % width_z
        spots[s, 0] = spot // (width_y * width_z) + HALO - slab * depth
        spots[s, 1] = z % chunks
        spots[s, 2] = y % groups
        spots[s, 3] = y // groups
        spots[s, 4] = z // chunks


def forward_sweep(part, spots, coef, src, dst, t, depth, together):
    parity = lax.axis_index("vox") % 2
    first, planes = part(t, depth, parity)
    sweep_planes(coef, src, dst, first, planes, None, together)
    for s in range(src.shape[0]):
        at = spots[s, 0]

        @pl.when(jnp.logical_and(at >= first, at < first + planes))
        def _():
            where = (spots[s, 1], pl.ds(pl.multiple_of(spots[s, 2] * SUB, SUB), SUB), slice(None))
            inverse = coef[(6, at - (HALO - SWEEPS), *where)]
            hit = jnp.logical_and(sub_ids() == spots[s, 3], lane_ids() == spots[s, 4])
            dst[(s, at, *where)] = dst[(s, at, *where)] + jnp.where(hit, source_gain * inverse, 0.0)


def early_sweeps(sweep, one, two, begin):
    for t in range(begin, SWEEPS):
        src, dst = (one, two) if t % 2 == 0 else (two, one)
        sweep(early_part, src, dst, t, 4)


def late_sweeps(sweep, one, two):
    def step(i, carry):
        sweep(late_part, one, two, 2 * i, HALO)
        sweep(late_part, two, one, 2 * i + 1, HALO)
        return carry

    lax.fori_loop(0, SWEEPS // 2, step, 0)


def early_kernel(positions, coef_own, own, near, coef, one, two, kap, mu, spots):
    count, depth = own.shape[:2]
    slab = lax.axis_index("vox")
    parity = slab % 2
    copy_planes(coef_own, (0,), 0, kap, (), HALO, depth, 0.5)
    copy_planes(near, (), 0, kap, (), halo_place(parity, True, depth, HALO), HALO, 0.5)
    copy_planes(coef_own, (1,), 0, mu, (), SWEEPS, depth)
    copy_planes(near, (), HALO, mu, (), halo_place(parity, True, depth, SWEEPS), SWEEPS)
    coefficient_planes(slab, kap, mu, coef, *early_part(0, depth, parity), depth)
    for s in range(count):
        copy_planes(own, (s,), 0, one, (s,), HALO, depth)
        copy_planes(near, (), HALO + SWEEPS + s * HALO, one, (s,), halo_place(parity, True, depth, HALO), HALO)
    find_sources(positions, spots, count, depth, *own.shape[2:4])

    def sweep(part, src, dst, t, together):
        forward_sweep(part, spots, coef, src, dst, t, depth, together)

    early_sweeps(sweep, one, two, 0)


def forward_kernel(positions, one_in, two_in, coef_in, coef_own, far, *rest):
    totals, (cells, one, two, coef, forward, adjoint_source, kap, mu, spots) = rest[:-9], rest[-9:]
    count, planes, chunks, width_y = one.shape[:4]
    depth = planes - 2 * HALO
    width_z, groups = chunks * LANES, width_y // SUB
    slab = lax.axis_index("vox")
    parity = slab % 2
    edge = jnp.where(parity == 0, 0, depth - 2)
    copy_planes(coef_own, (0,), edge, kap, (), edge + HALO, 2, 0.5)
    copy_planes(far, (), 0, kap, (), halo_place(parity, False, depth, HALO), HALO, 0.5)
    copy_planes(coef_own, (1,), edge, mu, (), edge + SWEEPS, 2)
    copy_planes(far, (), HALO, mu, (), halo_place(parity, False, depth, SWEEPS), SWEEPS)
    coefficient_planes(slab, kap, mu, coef, *late_part(0, depth, parity), depth)
    for s in range(count):
        copy_planes(far, (), HALO + SWEEPS + s * HALO, one, (s,), halo_place(parity, False, depth, HALO), HALO)
    find_sources(positions, spots, count, depth, chunks, width_y)

    def sweep(part, src, dst, t, together):
        forward_sweep(part, spots, coef, src, dst, t, depth, together)

    late_sweeps(sweep, one, two)
    for s in range(count):
        copy_planes(one, (s,), HALO, forward, (s,), 0, depth + 1)
    local_cells = cells[...] - slab * (depth * width_y * width_z)
    row_mask, z_hot = detector_masks(local_cells, 0, depth, width_y, width_z)
    total = sum(part[...] for part in totals)
    for s in range(count):
        field = [one[s, pl.ds(HALO, depth), j].reshape(depth * width_y, LANES) for j in range(chunks)]
        sampled = exact_dot(jnp.concatenate(field, axis=1), jnp.concatenate(z_hot, axis=0), 0)
        predicted = jnp.sum(jnp.where(row_mask, sampled, 0.0), axis=0, keepdims=True)
        adjoint_source[pl.ds(s, 1), :] = predicted * total[s : s + 1] - total[count + s : count + s + 1]
    adjoint_source[pl.ds(count, 1), :] = local_cells.astype(jnp.float32)


def adjoint_first_kernel(coef, own, near, two, one):
    count, depth = own.shape[:2]
    parity = lax.axis_index("vox") % 2
    for s in range(count):
        copy_planes(own, (s,), 0, one, (s,), HALO, depth)
        copy_planes(near, (), s * HALO, one, (s,), halo_place(parity, True, depth, HALO), HALO)
    sweep_planes(coef, one, two, *early_part(0, depth, parity), None)


def add_sources(coef, source, bias, at, planes, moved, swept=None):
    count, unused, chunks, width_y, lanes = bias.shape
    width_z = chunks * LANES
    cells = source[pl.ds(count, 1), :].astype(jnp.int32) + moved * (width_y * width_z)
    row_mask, z_hot = detector_masks(cells, at, planes, width_y, width_z)
    for s in range(count):
        spreads = [jnp.where(row_mask, part.astype(jnp.float32), 0.0).astype(jnp.bfloat16) for part in split(source[pl.ds(s, 1), :])]
        for j in range(chunks):
            placed = 0.0
            for spread in spreads:
                placed = placed + lax.dot_general(spread, z_hot[j], (((1,), (1,)), ((), ())), preferred_element_type=jnp.float32)
            placed = placed.reshape(planes, width_y, LANES)
            placed = placed * coef[6, pl.ds(at, planes), j, pl.ds(0, width_y)]
            bias[s, pl.ds(at, planes), j] = placed
            if swept is not None:
                place = pl.ds(at + (HALO - SWEEPS), planes)
                swept[s, place, j] = swept[s, place, j] + placed


def adjoint_early_kernel(two_in, coef, source, near_source, two, one, bias):
    count, planes, chunks, width_y = one.shape[:4]
    depth = planes - 2 * HALO
    parity = lax.axis_index("vox") % 2
    moved = SWEEPS + jnp.where(parity == 0, depth, -depth)
    add_sources(coef, near_source, bias, halo_place(parity, True, depth, SWEEPS), SWEEPS, moved, two)
    add_sources(coef, source, bias, SWEEPS, depth, SWEEPS, two)

    def sweep(part, src, dst, t, together):
        sweep_planes(coef, src, dst, *part(t, depth, parity), bias, together)

    early_sweeps(sweep, one, two, 1)


def places(order):
    found = [0]
    for bit in reversed(order):
        found = found + [place | 1 << bit for place in found]
    return found


def adjoint_kernel(orders, one_in, two_in, bias_in, coef, own, far, forward, far_source, one, two, bias, *rest):
    outs, plane_outs = rest[:-2], rest[-2:]
    count, planes, chunks, width_y = one.shape[:4]
    depth = planes - 2 * HALO
    groups = width_y // SUB
    parity, group = lax.axis_index("vox") % 2, lax.axis_index("src")
    for s in range(count):
        copy_planes(far, (), s * HALO, one, (s,), halo_place(parity, False, depth, HALO), HALO)
        edge = jnp.where(parity == 0, 0, depth - 2)
        copy_planes(own, (s,), edge, one, (s,), edge + HALO, 2)
    moved = SWEEPS - jnp.where(parity == 0, depth, -depth)
    add_sources(coef, far_source, bias, halo_place(parity, False, depth, SWEEPS), SWEEPS, moved)

    def sweep(part, src, dst, t, together):
        sweep_planes(coef, src, dst, *part(t, depth, parity), bias, together)

    late_sweeps(sweep, one, two)
    src = one
    lane, sub = lane_ids(), sub_ids()

    def steps(ref, s, at, mids, g):
        mid = mids[g]
        high = load_rows(ref, (s, at + 1), g, chunks)
        after = next_y(mids, g)
        if g + 1 == groups:
            after = [jnp.where(sub == SUB - 1, 0.0, c) for c in after]
        right = next_z(mid)
        right[-1] = jnp.where(lane == LANES - 1, 0.0, right[-1])
        return [[other[j] - mid[j] for j in range(chunks)] for other in (high, after, right)]

    tiles = 1 << len(orders[0])
    tile_rows = width_y // tiles

    def plane(p, plane_out):
        mids_f = [load_plane(forward, (s, p), groups, chunks) for s in range(count)]
        mids_a = [load_plane(src, (s, p + HALO), groups, chunks) for s in range(count)]
        for g in range(groups):
            mua_sum, kappa_sum = [0.0] * chunks, [0.0] * chunks
            for s in range(count):
                d_f = steps(forward, s, p, mids_f[s], g)
                d_a = steps(src, s, p + HALO, mids_a[s], g)
                for j in range(chunks):
                    mua_sum[j] = mua_sum[j] - mids_f[s][g][j] * mids_a[s][g][j]
                    for a, b in zip(d_f, d_a):
                        kappa_sum[j] = kappa_sum[j] - a[j] * b[j]
            for j in range(chunks):
                plane_out[0, j, pl.ds(g, SUB, stride=groups), :] = mua_sum[j]
                plane_out[1, j, pl.ds(g, SUB, stride=groups), :] = kappa_sum[j]
        for k, order in enumerate(orders):
            for i, place in enumerate(places(order)):
                out = outs[2 * k + (0 if i < tiles // 2 else 1)]
                first = pl.multiple_of((group ^ place) * tile_rows, SUB)
                for j in range(chunks):
                    out[i % (tiles // 2), p, j] = plane_out[k, j, pl.ds(first, tile_rows), :]

    def pair(i, carry):
        plane(2 * i, plane_outs[0])
        plane(2 * i + 1, plane_outs[1])
        return carry

    lax.fori_loop(0, depth // 2, pair, 0)


def unpack_kernel(*refs):
    pairs, outs = refs[: -len(refs) // 3], refs[-(len(refs) // 3) :]
    depth, chunks, rows, lanes = pairs[0].shape
    order = z_order(chunks * LANES, 1)
    for k, out in enumerate(outs):
        total = pairs[2 * k][...] + pairs[2 * k + 1][...]
        total = jnp.concatenate([total[:, j].reshape(depth * rows, LANES) for j in range(chunks)], axis=1)
        natural = exact_dot(total, order, 0)
        out[...] = natural.reshape(out.shape)


def measured_kernel(count, sources, detectors, data, weight, *outs):
    kinds, detector_count = outs[0].shape
    chunks, width = sources.shape
    total = jnp.zeros((len(outs) * kinds, detector_count), jnp.float32)
    detector_at = lax.broadcasted_iota(jnp.int32, (detector_count, width), 0) + lax.axis_index("vox") * detector_count
    kind_at = lax.broadcasted_iota(jnp.int32, (len(outs) * kinds, width), 0)
    source_at = (kind_at // kinds ^ lax.axis_index("src")) * count + kind_at % count
    with_data = kind_at % kinds >= count
    for i in range(chunks):
        row = pl.ds(i, 1)
        hot = (detector_at == detectors[row, :]).astype(jnp.bfloat16)
        w = weight[row, :]
        left = jnp.where(source_at == sources[row, :], jnp.where(with_data, w * data[row, :], w), 0.0)
        for part in split(left):
            total = total + lax.dot_general(part, hot, (((1,), (1,)), ((), ())), preferred_element_type=jnp.float32)
    for d, out in enumerate(outs):
        out[...] = total[d * kinds : (d + 1) * kinds]


VMEM = pl.BlockSpec(memory_space=pltpu.VMEM)
SMEM = pl.BlockSpec(memory_space=pltpu.SMEM)


def held(*shape):
    return pltpu.VMEM(shape, jnp.float32)


def call(kernel, outs, scratch, limit, *args, raw=(), fetched=(), positions=None, kept=0, after=()):
    args = [pltpu.with_memory_space_constraint(a, pltpu.VMEM) for a in args]
    args += [pltpu.with_memory_space_constraint(a, pltpu.HBM) for a in raw]
    specs = [VMEM] * len(args)
    args += [pltpu.with_memory_space_constraint(a, pltpu.HBM) for a in fetched]
    specs += [pl.BlockSpec(memory_space=pltpu.HBM)] * len(fetched)
    if after:
        inner, used = kernel, len(args) + (positions is not None)
        kernel = lambda *refs: inner(*refs[:used], *refs[used + len(after) :])
        args += [pltpu.with_memory_space_constraint(a, pltpu.VMEM) for a in after]
        specs += [VMEM] * len(after)
    shift = 0
    if positions is not None:
        args, specs = [positions, *args], [SMEM, *specs]
        shift = 1
    return pl.pallas_call(
        kernel,
        out_shape=outs,
        in_specs=specs,
        out_specs=[VMEM] * len(outs),
        scratch_shapes=scratch,
        input_output_aliases={k + shift: k for k in range(kept)},
        compiler_params=pltpu.CompilerParams(vmem_limit_bytes=limit * 1024 * 1024),
        cost_estimate=pl.CostEstimate(flops=1, bytes_accessed=1, transcendentals=0),
    )(*args)


def near_swap(block, count):
    return lax.ppermute(block, "vox", [(i, i ^ 1) for i in range(count) if i ^ 1 < count])


def far_swap(block, count):
    pairs = [(i, i + 1) for i in range(1, count - 1, 2)]
    return lax.ppermute(block, "vox", pairs + [(b, a) for a, b in pairs])


def body(
    kappa,
    mua,
    prior_forward_fields,
    prior_adjoint_fields,
    source_position,
    detector_voxel,
    measured_source,
    measured_detector,
    measured_data,
    measured_weight,
):
    count, depth, width_y, width_z = prior_forward_fields.shape
    slabs, groups = lax.axis_size("vox"), lax.axis_size("src")
    detectors = detector_voxel.shape[0]
    f32 = jnp.float32
    plane = (width_z // LANES, width_y, LANES)

    def pack(kinds, *blocks, after=()):
        rim = held(sum(sum(widths) for widths in kinds), *plane)
        outs = [held(len(widths), depth, *plane) for widths in kinds] + [rim, rim]
        blocks_held = sum(len(widths) for widths in kinds)
        scratch = [held(blocks_held, depth, width_y, width_z), pltpu.SemaphoreType.DMA((blocks_held,))]
        return call(functools.partial(pack_kernel, kinds), outs, scratch, 6, fetched=blocks, after=after)

    def sides(near, far):
        return near_swap(near, slabs), far_swap(far, slabs)

    planes = depth + 2 * HALO
    field = held(count, planes, *plane)
    padded = (plane[0], width_y + SUB, LANES)
    coef_held = held(7, planes - 2, *padded)
    coef_work = [held(planes, *plane), held(planes - 2, *plane)]

    field_rims = (HALO,) * count
    coef_own, fwd_own, near, far = pack([(HALO, SWEEPS), field_rims], kappa, mua, prior_forward_fields)
    near, far = sides(near, far)
    adj_own, adj_near, adj_far = pack([field_rims], prior_adjoint_fields, after=[near])
    adj_near, adj_far = sides(adj_near, adj_far)
    coef, one, two = call(
        early_kernel,
        [coef_held, field, field],
        [*coef_work, pltpu.SMEM((count, 5), jnp.int32)],
        6,
        coef_own,
        fwd_own,
        near,
        positions=source_position,
        after=[adj_near],
    )
    rows = measured_source.shape[0]
    sums = call(
        functools.partial(measured_kernel, count),
        [held(2 * count, detectors)] * groups,
        [],
        2,
        raw=[a.reshape(rows // LANES, LANES) for a in (measured_source, measured_detector, measured_data, measured_weight)],
        after=[adj_near],
    )
    totals = [sums[0]] + [lax.ppermute(sums[d], "src", [(i, i ^ d) for i in range(groups)]) for d in range(1, groups)]
    (adj_two,) = call(adjoint_first_kernel, [field], [field], 10, coef, adj_own, adj_near)
    unused, unused, coef, forward, source = call(
        forward_kernel,
        [field, field, coef_held, held(count, depth + 1, *plane), held(count + 1, detectors)],
        [*coef_work, pltpu.SMEM((count, 5), jnp.int32)],
        6,
        one,
        two,
        coef,
        coef_own,
        far,
        *totals,
        raw=[detector_voxel.reshape(1, detectors)],
        positions=source_position,
        kept=3,
        after=[adj_two],
    )
    source_near, source_far = sides(source, source)
    two, one, bias = call(
        adjoint_early_kernel,
        [field, field, held(count, planes - 2, *plane)],
        [],
        6,
        adj_two,
        coef,
        source,
        source_near,
        kept=1,
    )
    bits = list(range(groups.bit_length() - 1))
    orders = (bits, bits[::-1])
    half = held(groups // 2, depth, plane[0], width_y // groups, LANES)
    unused, unused, unused, *parts = call(
        functools.partial(adjoint_kernel, orders),
        [field, field, held(count, planes - 2, *plane)] + [half] * 4,
        [held(2, *plane)] * 2,
        6,
        one,
        two,
        bias,
        coef,
        adj_own,
        adj_far,
        forward,
        source_far,
        kept=3,
    )

    def swap(block, bit):
        return lax.ppermute(block, "src", [(i, i ^ 1 << bit) for i in range(groups)])

    kept, sent = [parts[0], parts[2]], [parts[1], parts[3]]
    for step in range(len(bits)):
        got = [swap(sent[k], orders[k][step]) for k in range(2)]
        if step + 1 < len(bits):
            total = [kept[k] + got[k] for k in range(2)]
            middle = total[0].shape[0] // 2
            kept, sent = [t[:middle] for t in total], [t[middle:] for t in total]
    tile = jax.ShapeDtypeStruct((depth, width_y // groups, width_z), f32)
    return tuple(call(unpack_kernel, [tile, tile], [], 3, kept[0][0], got[0][0], kept[1][0], got[1][0]))


def solution(mesh):
    in_specs = (
        P("vox", None, None),
        P("vox", None, None),
        P("src", "vox", None, None),
        P("src", "vox", None, None),
        P(),
        P("vox"),
        P(("src", "vox")),
        P(("src", "vox")),
        P(("src", "vox")),
        P(("src", "vox")),
    )
    out_specs = (P("vox", "src", None), P("vox", "src", None))
    return jax.shard_map(body, mesh=mesh, in_specs=in_specs, out_specs=out_specs, check_vma=False)
```

```python
import functools

import jax
import jax.numpy as jnp
from jax import lax
from jax.experimental import pallas as pl
from jax.experimental.pallas import tpu as pltpu
from jax.sharding import PartitionSpec as P

SWEEPS = 6
HALO = SWEEPS + 1
LANES = 128
SUB = 8

source_gain = 10.0


def lane_ids():
    return lax.broadcasted_iota(jnp.int32, (SUB, LANES), 1)


def sub_ids():
    return lax.broadcasted_iota(jnp.int32, (SUB, LANES), 0)


def next_z(chunks):
    return chunks[1:] + [pltpu.roll(chunks[0], LANES - 1, 1)]


def prev_z(chunks):
    return [pltpu.roll(chunks[-1], 1, 1)] + chunks[:-1]


def next_y(rows, g):
    return rows[g + 1] if g + 1 < len(rows) else [pltpu.roll(c, SUB - 1, 0) for c in rows[0]]


def prev_y(rows, g):
    return rows[g - 1] if g > 0 else [pltpu.roll(c, 1, 0) for c in rows[-1]]


def load_rows(ref, lead, g, chunks):
    return [ref[(*lead, j, pl.ds(SUB * g, SUB), slice(None))] for j in range(chunks)]


def load_plane(ref, lead, groups, chunks):
    return [load_rows(ref, lead, g, chunks) for g in range(groups)]


def store_rows(ref, lead, g, values):
    for j, value in enumerate(values):
        ref[(*lead, j, pl.ds(SUB * g, SUB), slice(None))] = value


def copy_planes(src, src_lead, src_first, dst, dst_lead, dst_first, count, scale=None):
    for i in range(count):
        plane = src[(*src_lead, src_first + i)]
        dst[(*dst_lead, dst_first + i)] = plane if scale is None else scale * plane


def split(values):
    high = values.astype(jnp.bfloat16)
    return high, (values - high.astype(jnp.float32)).astype(jnp.bfloat16)


def exact_dot(values, hot, hot_dim):
    dims = (((1,), (hot_dim,)), ((), ()))
    return sum(lax.dot_general(part, hot, dims, preferred_element_type=jnp.float32) for part in split(values))


def z_order(width_z, natural_dim):
    chunks = width_z // LANES
    z = lax.broadcasted_iota(jnp.int32, (width_z, width_z), natural_dim)
    place = lax.broadcasted_iota(jnp.int32, (width_z, width_z), 1 - natural_dim)
    return (z == place % LANES * chunks + place // LANES).astype(jnp.bfloat16)


def pack_kernel(kinds, *refs):
    (far, buffers, arrived), refs = refs[-3:], refs[:-3]
    owns, fetched = refs[-len(kinds) :], refs[: -len(kinds)]
    copies, first = [], 0
    for n, ref in enumerate(fetched):
        here = first if len(ref.shape) == 3 else pl.ds(first, ref.shape[0])
        copies.append((first, pltpu.make_async_copy(ref, buffers.at[here], arrived.at[n])))
        first += 1 if len(ref.shape) == 3 else ref.shape[0]
    for unused, copy in copies:
        copy.start()
    blocks = list(range(buffers.shape[0]))
    depth, width_y, width_z = buffers.shape[1:]
    chunks, groups = width_z // LANES, width_y // SUB
    parity = lax.axis_index("vox") % 2
    order = z_order(width_z, 0)
    together = 4
    at = 0
    for own, widths in zip(owns, kinds):
        for b, width in enumerate(widths):
            if copies and copies[0][0] == blocks[0]:
                copies.pop(0)[1].wait()
            block = buffers.at[blocks.pop(0)]
            for first in range(0, depth, together):
                values = block[pl.ds(first, together)].reshape(together * width_y, width_z)
                packed = exact_dot(values, order, 0)
                for i in range(together):
                    for y in range(0, width_y, SUB):
                        for j in range(chunks):
                            part = packed[i * width_y + y : i * width_y + y + SUB, LANES * j : LANES * (j + 1)]
                            if groups == SUB:
                                own[b, first + i, j, pl.ds(y // SUB, SUB, stride=SUB), :] = part
                            else:
                                for k in range(SUB):
                                    row = (y + k) % groups * SUB + (y + k) // groups
                                    own[b, first + i, j, pl.ds(row, 1), :] = part[k : k + 1]
            low, high = 0, depth - width
            copy_planes(own, (b,), jnp.where(parity == 0, low, high), far, (), at, width)
            at += width


def near_planes(near, lead, width, dst, dst_lead, dst_first, parity, scale=None):
    first = jnp.where(parity == 0, 0, near.shape[1] - width)
    copy_planes(near, lead, first, dst, dst_lead, dst_first, width, scale)


def early_part(t, depth, parity):
    planes = depth + HALO - 2 - 2 * t
    more = 1 if t > 0 and planes % 4 == 3 else 0
    return jnp.where(parity == 0, HALO + 1 + t, 1 + t - more), planes + more


def late_part(t, depth, parity):
    return jnp.where(parity == 0, 1 + t, depth + HALO - 1 - t), HALO


def halo_place(parity, near, depth, width):
    return jnp.where((parity == 0) == near, width + depth, 0)


def coefficient_planes(slab, kap, mu, out, first, count, depth):
    chunks, width_y = kap.shape[1:3]
    groups = width_y // SUB
    lane, sub = lane_ids(), sub_ids()
    grid_planes = lax.axis_size("vox") * depth

    def plane(n, carry):
        at = first + n
        i = at - (HALO - SWEEPS)
        place = slab * depth + i
        inside = jnp.logical_and(place >= SWEEPS, place < grid_planes + SWEEPS)
        rows = load_plane(kap, (at,), groups, chunks)
        for g in range(groups):
            mid = rows[g]
            low = load_rows(kap, (at - 1,), g, chunks)
            high = load_rows(kap, (at + 1,), g, chunks)
            before, after = prev_y(rows, g), next_y(rows, g)
            if g == 0:
                before = [jnp.where(sub == 0, 0.0, c) for c in before]
            if g + 1 == groups:
                after = [jnp.where(sub == SUB - 1, 0.0, c) for c in after]
            left, right = prev_z(mid), next_z(mid)
            left[0] = jnp.where(lane == 0, 0.0, left[0])
            right[-1] = jnp.where(lane == LANES - 1, 0.0, right[-1])
            absorb = load_rows(mu, (i,), g, chunks)
            for j in range(chunks):
                face = [mid[j] + other[j] for other in (low, high, before, after, left, right)]
                diagonal = absorb[j] + face[0] + face[1] + face[2] + face[3] + face[4] + face[5]
                inverse = jnp.where(inside, 1.0 / diagonal, 0.0)
                if g == 0:
                    face[2] = jnp.where(sub == 0, 0.0, face[2])
                if g + 1 == groups:
                    face[3] = jnp.where(sub == SUB - 1, 0.0, face[3])
                if j == 0:
                    face[4] = jnp.where(lane == 0, 0.0, face[4])
                if j + 1 == chunks:
                    face[5] = jnp.where(lane == LANES - 1, 0.0, face[5])
                for k in range(6):
                    out[k, i, j, pl.ds(SUB * g, SUB), :] = face[k] * inverse
                out[6, i, j, pl.ds(SUB * g, SUB), :] = inverse
        return carry

    lax.fori_loop(0, count, plane, 0)


def sweep_planes(coef, src, dst, first, planes, bias, together=4):
    count, unused, chunks, width_y, lanes = src.shape
    groups = width_y // SUB

    def one(at):
        c_at = at - (HALO - SWEEPS)
        for g in range(groups):
            faces = [load_rows(coef, (k, c_at), g, chunks) for k in range(6)]
            for s in range(count):
                rows = {h: load_rows(src, (s, at), h % groups, chunks) for h in (g - 1, g, g + 1)}
                mid = rows[g]
                low = load_rows(src, (s, at - 1), g, chunks)
                high = load_rows(src, (s, at + 1), g, chunks)
                before = rows[g - 1] if g > 0 else [pltpu.roll(c, 1, 0) for c in rows[g - 1]]
                after = rows[g + 1] if g + 1 < groups else [pltpu.roll(c, SUB - 1, 0) for c in rows[g + 1]]
                left, right = prev_z(mid), next_z(mid)
                result = []
                for j in range(chunks):
                    total = faces[0][j] * low[j] + faces[1][j] * high[j]
                    total = total + (faces[2][j] * before[j] + faces[3][j] * after[j])
                    total = total + (faces[4][j] * left[j] + faces[5][j] * right[j])
                    result.append(total)
                if bias is not None:
                    extra = load_rows(bias, (s, c_at), g, chunks)
                    result = [a + b for a, b in zip(result, extra)]
                store_rows(dst, (s, at), g, result)

    def several(i, carry):
        for k in range(together):
            one(first + together * i + k)
        return carry

    if planes >= together:
        lax.fori_loop(0, planes // together, several, 0)
    for k in range(planes // together * together, planes):
        one(first + k)


def detector_masks(cells, first, planes, width_y, width_z):
    groups, chunks = width_y // SUB, width_z // LANES
    y, z = cells // width_z % width_y, cells % width_z
    row = (cells // (width_y * width_z) - first) * width_y + y % groups * SUB + y // groups
    row_at = lax.broadcasted_iota(jnp.int32, (planes * width_y, cells.shape[1]), 0)
    lane_at = lax.broadcasted_iota(jnp.int32, (LANES, cells.shape[1]), 0)
    return row_at == row, [(lane_at * chunks + j == z).astype(jnp.bfloat16) for j in range(chunks)]


def find_sources(positions, spots, count, depth, chunks, width_y):
    width_z, groups = chunks * LANES, width_y // SUB
    slab, group = lax.axis_index("vox"), lax.axis_index("src")
    for s in range(count):
        spot = positions[group * count + s]
        y, z = spot // width_z % width_y, spot % width_z
        spots[s, 0] = spot // (width_y * width_z) + HALO - slab * depth
        spots[s, 1] = z % chunks
        spots[s, 2] = y % groups
        spots[s, 3] = y // groups
        spots[s, 4] = z // chunks


def forward_sweep(part, spots, coef, src, dst, t, depth, together):
    parity = lax.axis_index("vox") % 2
    first, planes = part(t, depth, parity)
    sweep_planes(coef, src, dst, first, planes, None, together)
    for s in range(src.shape[0]):
        at = spots[s, 0]

        @pl.when(jnp.logical_and(at >= first, at < first + planes))
        def _():
            where = (spots[s, 1], pl.ds(pl.multiple_of(spots[s, 2] * SUB, SUB), SUB), slice(None))
            inverse = coef[(6, at - (HALO - SWEEPS), *where)]
            hit = jnp.logical_and(sub_ids() == spots[s, 3], lane_ids() == spots[s, 4])
            dst[(s, at, *where)] = dst[(s, at, *where)] + jnp.where(hit, source_gain * inverse, 0.0)


def early_sweeps(sweep, one, two, begin):
    for t in range(begin, SWEEPS):
        src, dst = (one, two) if t % 2 == 0 else (two, one)
        sweep(early_part, src, dst, t, 4)


def late_sweeps(sweep, one, two):
    def step(i, carry):
        sweep(late_part, one, two, 2 * i, HALO)
        sweep(late_part, two, one, 2 * i + 1, HALO)
        return carry

    lax.fori_loop(0, SWEEPS // 2, step, 0)


def early_kernel(positions, coef_own, own, near_coef, near, coef, one, two, kap, mu, spots):
    count, depth = own.shape[:2]
    slab = lax.axis_index("vox")
    parity = slab % 2
    copy_planes(coef_own, (0,), 0, kap, (), HALO, depth, 0.5)
    near_planes(near_coef, (0,), HALO, kap, (), halo_place(parity, True, depth, HALO), parity, 0.5)
    copy_planes(coef_own, (1,), 0, mu, (), SWEEPS, depth)
    near_planes(near_coef, (1,), SWEEPS, mu, (), halo_place(parity, True, depth, SWEEPS), parity)
    coefficient_planes(slab, kap, mu, coef, *early_part(0, depth, parity), depth)
    for s in range(count):
        copy_planes(own, (s,), 0, one, (s,), HALO, depth)
        near_planes(near, (s,), HALO, one, (s,), halo_place(parity, True, depth, HALO), parity)
    find_sources(positions, spots, count, depth, *own.shape[2:4])

    def sweep(part, src, dst, t, together):
        forward_sweep(part, spots, coef, src, dst, t, depth, together)

    early_sweeps(sweep, one, two, 0)


def forward_kernel(positions, one_in, two_in, coef_in, coef_own, far, *rest):
    totals, (cells, one, two, coef, forward, adjoint_source, kap, mu, spots) = rest[:-9], rest[-9:]
    count, planes, chunks, width_y = one.shape[:4]
    depth = planes - 2 * HALO
    width_z, groups = chunks * LANES, width_y // SUB
    slab = lax.axis_index("vox")
    parity = slab % 2
    edge = jnp.where(parity == 0, 0, depth - 2)
    copy_planes(coef_own, (0,), edge, kap, (), edge + HALO, 2, 0.5)
    copy_planes(far, (), 0, kap, (), halo_place(parity, False, depth, HALO), HALO, 0.5)
    copy_planes(coef_own, (1,), edge, mu, (), edge + SWEEPS, 2)
    copy_planes(far, (), HALO, mu, (), halo_place(parity, False, depth, SWEEPS), SWEEPS)
    coefficient_planes(slab, kap, mu, coef, *late_part(0, depth, parity), depth)
    for s in range(count):
        copy_planes(far, (), HALO + SWEEPS + s * HALO, one, (s,), halo_place(parity, False, depth, HALO), HALO)
    find_sources(positions, spots, count, depth, chunks, width_y)

    def sweep(part, src, dst, t, together):
        forward_sweep(part, spots, coef, src, dst, t, depth, together)

    late_sweeps(sweep, one, two)
    for s in range(count):
        copy_planes(one, (s,), HALO, forward, (s,), 0, depth + 1)
    local_cells = cells[...] - slab * (depth * width_y * width_z)
    row_mask, z_hot = detector_masks(local_cells, 0, depth, width_y, width_z)
    total = sum(part[...] for part in totals)
    for s in range(count):
        field = [one[s, pl.ds(HALO, depth), j].reshape(depth * width_y, LANES) for j in range(chunks)]
        sampled = exact_dot(jnp.concatenate(field, axis=1), jnp.concatenate(z_hot, axis=0), 0)
        predicted = jnp.sum(jnp.where(row_mask, sampled, 0.0), axis=0, keepdims=True)
        adjoint_source[pl.ds(s, 1), :] = predicted * total[s : s + 1] - total[count + s : count + s + 1]
    adjoint_source[pl.ds(count, 1), :] = local_cells.astype(jnp.float32)


def adjoint_first_kernel(coef, own, near, two, one):
    count, depth = own.shape[:2]
    parity = lax.axis_index("vox") % 2
    for s in range(count):
        copy_planes(own, (s,), 0, one, (s,), HALO, depth)
        near_planes(near, (s,), HALO, one, (s,), halo_place(parity, True, depth, HALO), parity)
    sweep_planes(coef, one, two, *early_part(0, depth, parity), None)


def add_sources(coef, source, bias, at, planes, moved, swept=None):
    count, unused, chunks, width_y, lanes = bias.shape
    width_z = chunks * LANES
    cells = source[pl.ds(count, 1), :].astype(jnp.int32) + moved * (width_y * width_z)
    row_mask, z_hot = detector_masks(cells, at, planes, width_y, width_z)
    for s in range(count):
        spreads = [jnp.where(row_mask, part.astype(jnp.float32), 0.0).astype(jnp.bfloat16) for part in split(source[pl.ds(s, 1), :])]
        for j in range(chunks):
            placed = 0.0
            for spread in spreads:
                placed = placed + lax.dot_general(spread, z_hot[j], (((1,), (1,)), ((), ())), preferred_element_type=jnp.float32)
            placed = placed.reshape(planes, width_y, LANES)
            placed = placed * coef[6, pl.ds(at, planes), j, pl.ds(0, width_y)]
            bias[s, pl.ds(at, planes), j] = placed
            if swept is not None:
                place = pl.ds(at + (HALO - SWEEPS), planes)
                swept[s, place, j] = swept[s, place, j] + placed


def adjoint_early_kernel(two_in, coef, source, near_source, two, one, bias):
    count, planes, chunks, width_y = one.shape[:4]
    depth = planes - 2 * HALO
    parity = lax.axis_index("vox") % 2
    moved = SWEEPS + jnp.where(parity == 0, depth, -depth)
    add_sources(coef, near_source, bias, halo_place(parity, True, depth, SWEEPS), SWEEPS, moved, two)
    add_sources(coef, source, bias, SWEEPS, depth, SWEEPS, two)

    def sweep(part, src, dst, t, together):
        sweep_planes(coef, src, dst, *part(t, depth, parity), bias, together)

    early_sweeps(sweep, one, two, 1)


def places(order):
    found = [0]
    for bit in reversed(order):
        found = found + [place | 1 << bit for place in found]
    return found


def adjoint_kernel(orders, one_in, two_in, bias_in, coef, own, far, forward, far_source, one, two, bias, *rest):
    outs, plane_outs = rest[:-2], rest[-2:]
    count, planes, chunks, width_y = one.shape[:4]
    depth = planes - 2 * HALO
    groups = width_y // SUB
    parity, group = lax.axis_index("vox") % 2, lax.axis_index("src")
    for s in range(count):
        copy_planes(far, (), s * HALO, one, (s,), halo_place(parity, False, depth, HALO), HALO)
        edge = jnp.where(parity == 0, 0, depth - 2)
        copy_planes(own, (s,), edge, one, (s,), edge + HALO, 2)
    moved = SWEEPS - jnp.where(parity == 0, depth, -depth)
    add_sources(coef, far_source, bias, halo_place(parity, False, depth, SWEEPS), SWEEPS, moved)

    def sweep(part, src, dst, t, together):
        sweep_planes(coef, src, dst, *part(t, depth, parity), bias, together)

    late_sweeps(sweep, one, two)
    src = one
    lane, sub = lane_ids(), sub_ids()

    def steps(ref, s, at, mids, g):
        mid = mids[g]
        high = load_rows(ref, (s, at + 1), g, chunks)
        after = next_y(mids, g)
        if g + 1 == groups:
            after = [jnp.where(sub == SUB - 1, 0.0, c) for c in after]
        right = next_z(mid)
        right[-1] = jnp.where(lane == LANES - 1, 0.0, right[-1])
        return [[other[j] - mid[j] for j in range(chunks)] for other in (high, after, right)]

    tiles = 1 << len(orders[0])
    tile_rows = width_y // tiles

    def plane(p, plane_out):
        mids_f = [load_plane(forward, (s, p), groups, chunks) for s in range(count)]
        mids_a = [load_plane(src, (s, p + HALO), groups, chunks) for s in range(count)]
        for g in range(groups):
            mua_sum, kappa_sum = [0.0] * chunks, [0.0] * chunks
            for s in range(count):
                d_f = steps(forward, s, p, mids_f[s], g)
                d_a = steps(src, s, p + HALO, mids_a[s], g)
                for j in range(chunks):
                    mua_sum[j] = mua_sum[j] - mids_f[s][g][j] * mids_a[s][g][j]
                    for a, b in zip(d_f, d_a):
                        kappa_sum[j] = kappa_sum[j] - a[j] * b[j]
            for j in range(chunks):
                plane_out[0, j, pl.ds(g, SUB, stride=groups), :] = mua_sum[j]
                plane_out[1, j, pl.ds(g, SUB, stride=groups), :] = kappa_sum[j]
        for k, order in enumerate(orders):
            for i, place in enumerate(places(order)):
                out = outs[2 * k + (0 if i < tiles // 2 else 1)]
                first = pl.multiple_of((group ^ place) * tile_rows, SUB)
                for j in range(chunks):
                    out[i % (tiles // 2), p, j] = plane_out[k, j, pl.ds(first, tile_rows), :]

    def pair(i, carry):
        plane(2 * i, plane_outs[0])
        plane(2 * i + 1, plane_outs[1])
        return carry

    lax.fori_loop(0, depth // 2, pair, 0)


def unpack_kernel(*refs):
    pairs, outs = refs[: -len(refs) // 3], refs[-(len(refs) // 3) :]
    depth, chunks, rows, lanes = pairs[0].shape
    order = z_order(chunks * LANES, 1)
    for k, out in enumerate(outs):
        total = pairs[2 * k][...] + pairs[2 * k + 1][...]
        total = jnp.concatenate([total[:, j].reshape(depth * rows, LANES) for j in range(chunks)], axis=1)
        natural = exact_dot(total, order, 0)
        out[...] = natural.reshape(out.shape)


def measured_kernel(count, sources, detectors, data, weight, *outs):
    kinds, detector_count = outs[0].shape
    chunks, width = sources.shape
    total = jnp.zeros((len(outs) * kinds, detector_count), jnp.float32)
    detector_at = lax.broadcasted_iota(jnp.int32, (detector_count, width), 0) + lax.axis_index("vox") * detector_count
    kind_at = lax.broadcasted_iota(jnp.int32, (len(outs) * kinds, width), 0)
    source_at = (kind_at // kinds ^ lax.axis_index("src")) * count + kind_at % count
    with_data = kind_at % kinds >= count
    for i in range(chunks):
        row = pl.ds(i, 1)
        hot = (detector_at == detectors[row, :]).astype(jnp.bfloat16)
        w = weight[row, :]
        left = jnp.where(source_at == sources[row, :], jnp.where(with_data, w * data[row, :], w), 0.0)
        for part in split(left):
            total = total + lax.dot_general(part, hot, (((1,), (1,)), ((), ())), preferred_element_type=jnp.float32)
    for d, out in enumerate(outs):
        out[...] = total[d * kinds : (d + 1) * kinds]


VMEM = pl.BlockSpec(memory_space=pltpu.VMEM)
SMEM = pl.BlockSpec(memory_space=pltpu.SMEM)


def held(*shape):
    return pltpu.VMEM(shape, jnp.float32)


def call(kernel, outs, scratch, limit, *args, raw=(), fetched=(), positions=None, kept=0, after=()):
    args = [pltpu.with_memory_space_constraint(a, pltpu.VMEM) for a in args]
    args += [pltpu.with_memory_space_constraint(a, pltpu.HBM) for a in raw]
    specs = [VMEM] * len(args)
    args += [pltpu.with_memory_space_constraint(a, pltpu.HBM) for a in fetched]
    specs += [pl.BlockSpec(memory_space=pltpu.HBM)] * len(fetched)
    if after:
        inner, used = kernel, len(args) + (positions is not None)
        kernel = lambda *refs: inner(*refs[:used], *refs[used + len(after) :])
        args += [pltpu.with_memory_space_constraint(a, pltpu.VMEM) for a in after]
        specs += [VMEM] * len(after)
    shift = 0
    if positions is not None:
        args, specs = [positions, *args], [SMEM, *specs]
        shift = 1
    return pl.pallas_call(
        kernel,
        out_shape=outs,
        in_specs=specs,
        out_specs=[VMEM] * len(outs),
        scratch_shapes=scratch,
        input_output_aliases={k + shift: k for k in range(kept)},
        compiler_params=pltpu.CompilerParams(vmem_limit_bytes=limit * 1024 * 1024),
        cost_estimate=pl.CostEstimate(flops=1, bytes_accessed=1, transcendentals=0),
    )(*args)


def near_swap(block, count):
    return lax.ppermute(block, "vox", [(i, i ^ 1) for i in range(count) if i ^ 1 < count])


def far_swap(block, count):
    pairs = [(i, i + 1) for i in range(1, count - 1, 2)]
    return lax.ppermute(block, "vox", pairs + [(b, a) for a, b in pairs])


def body(
    kappa,
    mua,
    prior_forward_fields,
    prior_adjoint_fields,
    source_position,
    detector_voxel,
    measured_source,
    measured_detector,
    measured_data,
    measured_weight,
):
    count, depth, width_y, width_z = prior_forward_fields.shape
    slabs, groups = lax.axis_size("vox"), lax.axis_size("src")
    detectors = detector_voxel.shape[0]
    f32 = jnp.float32
    plane = (width_z // LANES, width_y, LANES)

    def pack(kinds, *blocks, after=()):
        rim = held(sum(sum(widths) for widths in kinds), *plane)
        outs = [held(len(widths), depth, *plane) for widths in kinds] + [rim]
        blocks_held = sum(len(widths) for widths in kinds)
        scratch = [held(blocks_held, depth, width_y, width_z), pltpu.SemaphoreType.DMA((blocks_held,))]
        *owns, far = call(functools.partial(pack_kernel, kinds), outs, scratch, 6, fetched=blocks, after=after)
        return *owns, *[near_swap(own, slabs) for own in owns], far_swap(far, slabs)

    def sides(near, far):
        return near_swap(near, slabs), far_swap(far, slabs)

    planes = depth + 2 * HALO
    field = held(count, planes, *plane)
    padded = (plane[0], width_y + SUB, LANES)
    coef_held = held(7, planes - 2, *padded)
    coef_work = [held(planes, *plane), held(planes - 2, *plane)]

    field_rims = (HALO,) * count
    coef_own, fwd_own, coef_near, near, far = pack([(HALO, SWEEPS), field_rims], kappa, mua, prior_forward_fields)
    adj_own, adj_near, adj_far = pack([field_rims], prior_adjoint_fields, after=[coef_near, near])
    coef, one, two = call(
        early_kernel,
        [coef_held, field, field],
        [*coef_work, pltpu.SMEM((count, 5), jnp.int32)],
        6,
        coef_own,
        fwd_own,
        coef_near,
        near,
        positions=source_position,
        after=[adj_near],
    )
    rows = measured_source.shape[0]
    sums = call(
        functools.partial(measured_kernel, count),
        [held(2 * count, detectors)] * groups,
        [],
        2,
        raw=[a.reshape(rows // LANES, LANES) for a in (measured_source, measured_detector, measured_data, measured_weight)],
        after=[adj_near],
    )
    totals = [sums[0]] + [lax.ppermute(sums[d], "src", [(i, i ^ d) for i in range(groups)]) for d in range(1, groups)]
    (adj_two,) = call(adjoint_first_kernel, [field], [field], 10, coef, adj_own, adj_near)
    unused, unused, coef, forward, source = call(
        forward_kernel,
        [field, field, coef_held, held(count, depth + 1, *plane), held(count + 1, detectors)],
        [*coef_work, pltpu.SMEM((count, 5), jnp.int32)],
        6,
        one,
        two,
        coef,
        coef_own,
        far,
        *totals,
        raw=[detector_voxel.reshape(1, detectors)],
        positions=source_position,
        kept=3,
        after=[adj_two],
    )
    source_near, source_far = sides(source, source)
    two, one, bias = call(
        adjoint_early_kernel,
        [field, field, held(count, planes - 2, *plane)],
        [],
        6,
        adj_two,
        coef,
        source,
        source_near,
        kept=1,
    )
    bits = list(range(groups.bit_length() - 1))
    orders = (bits, bits[::-1])
    half = held(groups // 2, depth, plane[0], width_y // groups, LANES)
    unused, unused, unused, *parts = call(
        functools.partial(adjoint_kernel, orders),
        [field, field, held(count, planes - 2, *plane)] + [half] * 4,
        [held(2, *plane)] * 2,
        6,
        one,
        two,
        bias,
        coef,
        adj_own,
        adj_far,
        forward,
        source_far,
        kept=3,
    )

    def swap(block, bit):
        return lax.ppermute(block, "src", [(i, i ^ 1 << bit) for i in range(groups)])

    kept, sent = [parts[0], parts[2]], [parts[1], parts[3]]
    for step in range(len(bits)):
        got = [swap(sent[k], orders[k][step]) for k in range(2)]
        if step + 1 < len(bits):
            total = [kept[k] + got[k] for k in range(2)]
            middle = total[0].shape[0] // 2
            kept, sent = [t[:middle] for t in total], [t[middle:] for t in total]
    tile = jax.ShapeDtypeStruct((depth, width_y // groups, width_z), f32)
    return tuple(call(unpack_kernel, [tile, tile], [], 3, kept[0][0], got[0][0], kept[1][0], got[1][0]))


def solution(mesh):
    in_specs = (
        P("vox", None, None),
        P("vox", None, None),
        P("src", "vox", None, None),
        P("src", "vox", None, None),
        P(),
        P("vox"),
        P(("src", "vox")),
        P(("src", "vox")),
        P(("src", "vox")),
        P(("src", "vox")),
    )
    out_specs = (P("vox", "src", None), P("vox", "src", None))
    return jax.shard_map(body, mesh=mesh, in_specs=in_specs, out_specs=out_specs, check_vma=False)
```
